32 devices in a mesh: dp: 4 (over x, core), seq: 8 (over z, y).
Axes of the slice: x: 2, y: 2, z: 4, core: 2. Of those that a mesh axis runs over, the one named last changes fastest.
Arguments:
- tokens: bfloat16 [12, 1024, 1536], P('dp', 'seq'), may hold values from -6 to 6
- cotangent: bfloat16 [12, 1024, 1536], P('dp', 'seq'), may hold values from -6 to 6
- lengths: int32 [12], P('dp'), may hold values from 256 to 1024, as said below
- in_weight: bfloat16 [1536, 4608], P(('dp', 'seq')), may hold values from -0.15625 to 0.15625
- conv_weight: bfloat16 [3, 1536], P(None, ('dp', 'seq')), may hold values from -3 to 3
- out_weight: bfloat16 [1536, 1536], P(('dp', 'seq')), may hold values from -0.15625 to 0.15625
- gain_one: bfloat16 [1536], P(('dp', 'seq')), may hold values from 0.099609375 to 1.8984375
- gain_two: bfloat16 [1536], P(('dp', 'seq')), may hold values from 0.099609375 to 1.8984375
- gate_weight: bfloat16 [1536, 6912], P(('dp', 'seq')), may hold values from -0.15625 to 0.15625
- up_weight: bfloat16 [1536, 6912], P(('dp', 'seq')), may hold values from -0.15625 to 0.15625
- down_weight: bfloat16 [6912, 1536], P(('dp', 'seq')), may hold values from -0.15625 to 0.15625
Outputs:
- mixed: bfloat16 [12, 1024, 1536], P('dp', 'seq')
- input_grad: float32 [12, 1024, 1536], P('dp', 'seq')
- in_grad: float32 [1536, 4608], P(('dp', 'seq'))
- conv_grad: float32 [3, 1536], P(None, ('dp', 'seq'))
- out_grad: float32 [1536, 1536], P(('dp', 'seq'))
- gain_one_grad: float32 [1536], P(('dp', 'seq'))
- gain_two_grad: float32 [1536], P(('dp', 'seq'))
- gate_grad: float32 [1536, 6912], P(('dp', 'seq'))
- up_grad: float32 [1536, 6912], P(('dp', 'seq'))
- down_grad: float32 [6912, 1536], P(('dp', 'seq'))
The draws below stay inside these ranges and needn't reach their ends.
Inputs may be any that keep to these rules, and one draw needn't show every extreme that they name: `lengths`: each slot's length is between 256 and 1024; in each aligned block of 3 slots one slot has length 1024.
All inputs are finite; a program needn't handle non-finite values.
Results may differ from the reference program's by a relative error of at most 0.0098.
Values may be sent and summed in bfloat16 or wider, within the bound.
No kernel may reach another device: no remote copies, remote signals or barrier semaphores. Data moves between devices by JAX's collectives and lax.ppermute only.
A program may use at most 512 MiB of HBM per device.

```python
import jax
import jax.numpy as jnp
from jax import lax

D = 1536
FF = 6912
SLOT_MB = 1
MICRO = 3
SEQ = 1024
SLOTS = 12


def draw_lengths(key, part):
    key = jax.random.fold_in(key, 11)
    group = MICRO * SLOT_MB
    groups = SLOTS // group
    drawn = jax.random.randint(jax.random.fold_in(key, 1), (SLOTS,), SEQ // 4, SEQ + 1)
    chosen = jax.random.randint(jax.random.fold_in(key, 2), (groups,), 0, group)
    index = jnp.arange(SLOTS, dtype=jnp.int32)
    owner = index // group
    inside = index % group
    full_slot = inside == jnp.take(chosen, owner)
    return jnp.where(full_slot, SEQ, drawn).astype(jnp.int32)


def block_levels(rng, shape, split, smallest, top_value):
    factor_of, own = 1.0, jax.random.fold_in(rng, 6)
    for axis_at, blocks in split:
        steps = jnp.exp(jax.random.uniform(jax.random.fold_in(own, axis_at), (blocks,), jnp.float32, smallest / len(split), top_value / len(split)))
        factor_of = factor_of * jnp.repeat(steps, shape[axis_at] // blocks).reshape([-1 if axis == axis_at else 1 for axis in range(len(shape))])
    return factor_of


def normal_values(stream_key, extent, deviation, most, pieces=(), held_as=jnp.bfloat16):
    entries = jax.random.normal(stream_key, extent, jnp.float32) * deviation
    if len(pieces) > 0:
        entries = block_levels(stream_key, extent, pieces, -0.22, 0.18) * entries
    return jnp.clip(entries, min=-most, max=most).astype(held_as)


def setup_inputs(seed: int = 0) -> dict:
    key_list = jax.random.split(jax.random.key(seed), 12)
    tokens = normal_values(key_list[0], (SLOTS, SEQ, D), 1.0, 6.0, ((0, 4), (1, 8)))
    cotangent = normal_values(key_list[1], (SLOTS, SEQ, D), 1.0, 6.0, ((0, 4), (1, 8)))
    lengths = draw_lengths(jax.random.fold_in(key_list[11], 71), 0)
    in_weight = normal_values(key_list[3], (D, 3 * D), D ** -0.5, 0.15625, ((0, 32),))
    conv_weight = normal_values(key_list[4], (3, D), 0.6, 3.0, ((1, 32),))
    out_weight = normal_values(key_list[5], (D, D), D ** -0.5, 0.15625, ((0, 32),))
    gain_one = jnp.clip(1.0 + 0.18 * jax.random.normal(key_list[6], (D,), jnp.float32), 0.099609375, 1.8984375).astype(jnp.bfloat16)
    gain_two = jnp.clip(1.0 + 0.18 * jax.random.normal(key_list[7], (D,), jnp.float32), 0.099609375, 1.8984375).astype(jnp.bfloat16)
    gate_weight = normal_values(key_list[8], (D, FF), D ** -0.5, 0.15625, ((0, 32),))
    up_weight = normal_values(key_list[9], (D, FF), D ** -0.5, 0.15625, ((0, 32),))
    down_weight = normal_values(key_list[10], (FF, D), (FF // 4) ** -0.5, 0.15625, ((0, 32),))
    return dict(tokens=tokens, cotangent=cotangent, lengths=lengths, in_weight=in_weight, conv_weight=conv_weight, out_weight=out_weight, gain_one=gain_one, gain_two=gain_two, gate_weight=gate_weight, up_weight=up_weight, down_weight=down_weight)


@jax.custom_vjp
def low(v):
    return lax.optimization_barrier(v.astype(jnp.bfloat16)).astype(jnp.float32)

@jax.custom_vjp
def low_back(v):
    return v

def low_keep(v):
    return (low(v), None)

def low_pass(kept, grad):
    return (grad,)

def back_keep(v):
    return (v, None)

def back_low(kept, grad):
    return (low(grad),)
low.defvjp(low_keep, low_pass)
low_back.defvjp(back_keep, back_low)

def matmul(left, right):
    return jnp.dot(left, right, precision=lax.Precision.HIGHEST, preferred_element_type=jnp.float32)

def rms_scale(values):
    return lax.rsqrt(lax.optimization_barrier(jnp.mean(values * values, axis=-1, keepdims=True)) + 1e-05)

def layer(inputs, mask, weights):
    in_weight, conv_weight, out_weight, gain_one, gain_two, gate_weight, up_weight, down_weight = weights
    width = inputs.shape[1]
    first_normalized = low(inputs * rms_scale(inputs) * gain_one)
    projected_triple = low_back(matmul(first_normalized, in_weight))
    b_part = projected_triple[:, :width]
    c_part = projected_triple[:, width:2 * width]
    x_part = projected_triple[:, 2 * width:]
    mixed_bx = b_part * x_part
    padded = jnp.concatenate([jnp.zeros((2, width), jnp.float32), mixed_bx], axis=0)
    conv = conv_weight[0] * padded[:-2] + conv_weight[1] * padded[1:-1] + conv_weight[2] * padded[2:]
    residual_branch = low(c_part * conv)
    mixer_output = low_back(matmul(residual_branch, out_weight))
    hidden_one = inputs + mixer_output
    second_normalized = low(hidden_one * rms_scale(hidden_one) * gain_two)
    gate_activation = low_back(matmul(second_normalized, gate_weight))
    upward_activation = low_back(matmul(second_normalized, up_weight))
    inner_product = low(jax.nn.silu(gate_activation) * upward_activation)
    feedforward_output = low_back(matmul(inner_product, down_weight))
    return mask * (hidden_one + feedforward_output)

def reference(tokens, cotangent, lengths, in_weight, conv_weight, out_weight, gain_one, gain_two, gate_weight, up_weight, down_weight):
    weights = tuple((w.astype(jnp.float32) for w in (in_weight, conv_weight, out_weight, gain_one, gain_two, gate_weight, up_weight, down_weight)))
    positions = jnp.arange(tokens.shape[1], dtype=jnp.int32)

    def step(totals, item):
        slot_in, slot_ct, length = item
        mask = (positions < length).astype(jnp.float32)[:, None]
        result, pull = jax.vjp(lambda a, w: layer(a, mask, w), slot_in.astype(jnp.float32), weights)
        d_input, d_weights = pull(slot_ct.astype(jnp.float32))
        totals = jax.tree.map(lambda s, g: s + g, totals, d_weights)
        return (totals, (result.astype(jnp.bfloat16), d_input))
    zeros = jax.tree.map(lambda w: jnp.zeros(w.shape, jnp.float32), weights)
    totals, (mixed, input_grad) = lax.scan(step, zeros, (tokens, cotangent, lengths))
    return (mixed, input_grad, totals[0], totals[1], totals[2], totals[3], totals[4], totals[5], totals[6], totals[7])
```

```python
import jax
import jax.numpy as jnp
from jax import lax
from jax.sharding import Mesh
from jax.sharding import PartitionSpec as P

BF = jnp.bfloat16
F32 = jnp.float32
GROUP = ("x", "c", "y")


def ring_of(count):
    return [0] + list(range(1, count, 2)) + list(range(count - 2 + count % 2, 0, -2))


def send(block, hop, sizes):
    nx, nc, ny = sizes
    dx, dc, dy = hop
    route = []
    for i in range(nx):
        for j in range(nc):
            for k in range(ny):
                source = (i * nc + j) * ny + k
                target = (((i + dx) % nx) * nc + (j + dc) % nc) * ny + (k + dy) % ny
                route.append((source, target))
    return lax.ppermute(block, GROUP, route)


def mirror(hop, sizes):
    return tuple((-h) % n for h, n in zip(hop, sizes))


def fetch(block, hop, sizes):
    return send(block, mirror(hop, sizes), sizes)


def group_gather(block, sizes):
    nx, nc, ny = sizes
    half = block.shape[0] // 2
    got = {(0, 0): block}
    for dx in range(1, nx):
        got[dx, 0] = fetch(block, (dx, 0, 0), sizes)
    for dy in range(1, ny):
        got[0, dy] = fetch(block, (0, 0, dy), sizes)
    for dx in range(1, nx):
        for dy in range(1, ny):
            one = fetch(got[dx, 0][:half], (0, 0, dy), sizes)
            two = fetch(got[0, dy][half:], (dx, 0, 0), sizes)
            got[dx, dy] = jnp.concatenate([one, two], axis=0)
    full = {}
    for (dx, dy), value in got.items():
        full[dx, 0, dy] = value
        for dc in range(1, nc):
            full[dx, dc, dy] = fetch(value, (0, dc, 0), sizes)
    return full


def group_reduce(parts, sizes):
    nx, nc, ny = sizes
    chip = {}
    for dx in range(nx):
        for dy in range(ny):
            total = parts[dx, 0, dy].astype(F32)
            for dc in range(1, nc):
                total = total + send(parts[dx, dc, dy].astype(BF), (0, dc, 0), sizes).astype(F32)
            chip[dx, dy] = total
    half = chip[0, 0].shape[0] // 2
    for dx in range(1, nx):
        for dy in range(1, ny):
            far = chip[dx, dy].astype(BF)
            one = send(far[:half], (dx, 0, 0), sizes).astype(F32)
            two = send(far[half:], (0, 0, dy), sizes).astype(F32)
            side = chip[0, dy]
            chip[0, dy] = jnp.concatenate([side[:half] + one, side[half:]], axis=0)
            side = chip[dx, 0]
            chip[dx, 0] = jnp.concatenate([side[:half], side[half:] + two], axis=0)
    total = chip[0, 0]
    for dx in range(1, nx):
        total = total + send(chip[dx, 0].astype(BF), (dx, 0, 0), sizes).astype(F32)
    for dy in range(1, ny):
        total = total + send(chip[0, dy].astype(BF), (0, 0, dy), sizes).astype(F32)
    return total


def group_exchange(parts, sizes):
    return {mirror(hop, sizes): send(value, hop, sizes) if any(hop) else value for hop, value in parts.items()}


class Line:
    def __init__(self, count):
        self.count = count
        self.ring = ring_of(count)
        self.route = [(self.ring[i], self.ring[(i + 1) % count]) for i in range(count)]
        place = {z: i for i, z in enumerate(self.ring)}
        table = [[self.ring[(place[z] - s) % count] for z in range(count)] for s in range(count + 1)]
        here = lax.axis_index("z")
        self.source = [here]
        for s in range(1, count + 1):
            at = jnp.int32(table[s][0])
            for z in range(1, count):
                at = jnp.where(here == z, jnp.int32(table[s][z]), at)
            self.source.append(at)

    def gather(self, block, axis):
        shape = list(block.shape)
        shape.insert(axis, self.count)
        full = jnp.zeros(shape, block.dtype)
        for s in range(self.count):
            if s > 0:
                block = lax.ppermute(block, "z", self.route)
            full = lax.dynamic_update_slice_in_dim(full, jnp.expand_dims(block, axis), self.source[s], axis)
        return full

    def reduce(self, parts, axis):
        total = None
        for s in range(1, self.count + 1):
            own = lax.dynamic_index_in_dim(parts, self.source[s], axis, keepdims=False).astype(F32)
            if total is None:
                total = own
            else:
                total = own + lax.ppermute(total.astype(BF), "z", self.route).astype(F32)
        return total


def dot(left, right):
    return jnp.dot(left, right, preferred_element_type=F32)


def dot_nt(left, right):
    return lax.dot_general(left, right, (((1,), (1,)), ((), ())), preferred_element_type=F32)


def dot_tn(left, right):
    return lax.dot_general(left, right, (((0,), (0,)), ((), ())), preferred_element_type=F32)


def rms_scale(values):
    return lax.rsqrt(jnp.mean(values * values, axis=-1, keepdims=True) + 1e-05)


def norm_back(gradient, values, scale, gain):
    scaled = gradient * gain
    mean_term = jnp.mean(scaled * values, axis=-1, keepdims=True)
    return scale * scaled - values * scale * scale * scale * mean_term


def on_device(
    tokens,
    cotangent,
    lengths,
    in_weight,
    conv_weight,
    out_weight,
    gain_one,
    gain_two,
    gate_weight,
    up_weight,
    down_weight,
):
    nx, nc, nz, ny = (lax.axis_size(name) for name in ("x", "c", "z", "y"))
    sizes = (nx, nc, ny)
    ndp = nx * nc
    slots, span, width = tokens.shape
    rows = slots * span
    own_in = in_weight.shape[0]
    own_hid = down_weight.shape[0]
    chan = nz * own_in
    hid = nz * own_hid
    hops = [(dx, dc, dy) for dx in range(nx) for dc in range(nc) for dy in range(ny)]
    sides = [(dx, dc) for dx in range(nx) for dc in range(nc)]
    line = Line(nz)
    row_y = lax.axis_index("y")
    first = (lax.axis_index("z") * ny + row_y) * span
    positions = first + jnp.arange(span, dtype=jnp.int32)
    mask = (positions[None, :] < lengths[:, None]).astype(F32).reshape(rows, 1)

    x_bf = tokens.reshape(rows, width)
    x = x_bf.astype(F32)
    d_out_bf = (mask * cotangent.reshape(rows, width).astype(F32)).astype(BF)

    gains = lax.all_gather(
        jnp.stack([gain_one, gain_two], axis=0), ("x", "c", "z", "y"), axis=1, tiled=True
    ).astype(F32)
    gain_a, gain_b = gains[0], gains[1]
    taps = line.gather(conv_weight, 1).reshape(3, chan).astype(F32)

    cut = in_weight.reshape(own_in, 3, ndp, nz, ny, own_in).transpose(2, 4, 0, 1, 3, 5)
    cut = cut.reshape(ndp * ny, own_in, 3 * chan)
    cut = lax.all_to_all(cut, GROUP, 0, 0, tiled=True).reshape(ndp, ny, own_in, 3 * chan)
    w_in = line.gather(cut, 1).reshape(width, 3 * chan)

    x_all = group_gather(x_bf, sizes)
    x_all = jnp.concatenate([x_all[h] for h in hops], axis=0).astype(F32)
    a_all = (x_all * rms_scale(x_all) * gain_a).astype(BF)

    w_out = line.gather(out_weight, 0).reshape(chan, width)
    w_out = group_gather(w_out, sizes)
    w_out = jnp.concatenate([w_out[h] for h in hops], axis=0)

    both = jnp.stack([gate_weight, up_weight], axis=1)
    both = both.reshape(own_in, 2, ndp, nz, ny, own_hid).transpose(2, 4, 0, 1, 3, 5)
    both = both.reshape(ndp * ny, own_in, 2 * hid)
    both = lax.all_to_all(both, GROUP, 0, 0, tiled=True).reshape(ndp, ny, own_in, 2 * hid)
    w_both = line.gather(both, 1).reshape(width, 2 * hid)
    w_down = line.gather(down_weight, 0).reshape(hid, width)

    bcx = dot(a_all, w_in)
    wide = (len(sides), ny, slots, span, chan)
    b_part = bcx[:, :chan].reshape(wide)
    c_part = bcx[:, chan : 2 * chan].reshape(wide)
    v_part = bcx[:, 2 * chan :].reshape(wide)
    bx = b_part * v_part
    even = row_y == 0
    tail = bx[:, :, :, -2:, :]
    over = lax.ppermute(jnp.where(even, tail[:, 1], tail[:, 0]), "z", [(i, i + 1) for i in range(nz - 1)])
    before = jnp.stack(
        [jnp.where(even, over, tail[:, 1]), jnp.where(even, tail[:, 0], over)], axis=1
    )
    padded = jnp.concatenate([before, bx], axis=3)
    past_two, past_one = padded[:, :, :, :-2], padded[:, :, :, 1:-1]
    conv = taps[0] * past_two + taps[1] * past_one + taps[2] * bx
    o_all = (c_part * conv).astype(BF).reshape(len(hops), rows, chan)
    o_own = group_exchange({h: o_all[i] for i, h in enumerate(hops)}, sizes)
    o_own = jnp.concatenate([o_own[h] for h in hops], axis=1)
    h1 = x + dot(o_own, w_out)
    scale_two = rms_scale(h1)
    a2 = (h1 * scale_two * gain_b).astype(BF)

    d_all = group_gather(d_out_bf, sizes)
    d_all = jnp.concatenate([d_all[h] for h in hops], axis=0)
    a2_all = group_gather(a2, sizes)
    a2_all = jnp.concatenate([a2_all[h] for h in hops], axis=0)
    gu = dot(a2_all, w_both)
    gate, up = gu[:, :hid], gu[:, hid:]
    sigma = jax.nn.sigmoid(gate)
    active = gate * sigma
    m = (active * up).astype(BF)
    dm = dot_nt(d_all, w_down)
    d_gate = (dm * up * sigma * (1.0 + gate * (1.0 - sigma))).astype(BF)
    d_up = (dm * active).astype(BF)
    d_both = jnp.concatenate([d_gate, d_up], axis=1)
    da2_part = dot_nt(d_both, w_both).reshape(len(hops), rows, width)
    f_part = dot(m, w_down).reshape(len(hops), rows, width)
    da2 = group_reduce({h: da2_part[i] for i, h in enumerate(hops)}, sizes)
    f = group_reduce({h: f_part[i] for i, h in enumerate(hops)}, sizes)
    mixed = (mask * (h1 + f)).astype(BF)

    down_grad = line.reduce(dot_tn(m, d_all).reshape(nz, own_hid, width), 0)
    both_part = dot_tn(a2_all, d_both).reshape(ndp, nz, ny, own_in, 2 * hid)
    both_sum = line.reduce(both_part, 1).astype(BF).reshape(ndp * ny, own_in, 2 * hid)
    both_sum = lax.all_to_all(both_sum, GROUP, 0, 0, tiled=True)
    both_sum = both_sum.reshape(ndp, ny, own_in, 2, nz, own_hid).transpose(3, 2, 0, 4, 1, 5)
    both_sum = both_sum.reshape(2, own_in, ndp * nz * ny * own_hid).astype(F32)
    gate_grad, up_grad = both_sum[0], both_sum[1]
    gain_two_grad = (
        jnp.sum(gate_grad * gate_weight.astype(F32) + up_grad * up_weight.astype(F32), axis=1)
        / gain_two.astype(F32)
    )

    dh1 = d_out_bf.astype(F32) + norm_back(da2, h1, scale_two, gain_b)
    datt = dh1.astype(BF)
    do_own = dot_nt(datt, w_out).astype(BF)
    do_all = group_exchange(
        {h: do_own[:, i * chan : (i + 1) * chan] for i, h in enumerate(hops)}, sizes
    )
    do_all = jnp.stack([do_all[h] for h in hops], axis=0).reshape(wide).astype(F32)
    out_part = dot_tn(o_own, datt).reshape(len(hops), chan, width)
    out_sum = group_reduce({h: out_part[i] for i, h in enumerate(hops)}, sizes)
    out_grad = line.reduce(out_sum.reshape(nz, own_in, width), 0)

    d_c = do_all * conv
    d_conv = do_all * c_part
    head = d_conv[:, :, :, :2, :]
    under = lax.ppermute(jnp.where(even, head[:, 0], head[:, 1]), "z", [(i + 1, i) for i in range(nz - 1)])
    after = jnp.stack(
        [jnp.where(even, head[:, 1], under), jnp.where(even, under, head[:, 0])], axis=1
    )
    padded_grad = jnp.concatenate([d_conv, after], axis=3)
    d_bx = (
        taps[2] * d_conv
        + taps[1] * padded_grad[:, :, :, 1:-1]
        + taps[0] * padded_grad[:, :, :, 2:]
    )
    all_rows = (0, 1, 2, 3)
    conv_part = jnp.stack(
        [
            jnp.sum(d_conv * past_two, axis=all_rows),
            jnp.sum(d_conv * past_one, axis=all_rows),
            jnp.sum(d_conv * bx, axis=all_rows),
        ],
        axis=0,
    )
    conv_grad = lax.psum_scatter(
        conv_part.reshape(3, nz, own_in), "z", scatter_dimension=1, tiled=True
    ).reshape(3, own_in)
    d_bcx = jnp.concatenate([d_bx * v_part, d_c, d_bx * b_part], axis=-1).astype(BF)
    d_bcx = d_bcx.reshape(len(hops) * rows, 3 * chan)
    da_part = dot_nt(d_bcx, w_in).reshape(len(hops), rows, width)
    da = group_reduce({h: da_part[i] for i, h in enumerate(hops)}, sizes)

    in_part = dot_tn(a_all, d_bcx).reshape(ndp, nz, ny, own_in, 3 * chan)
    in_sum = line.reduce(in_part, 1).astype(BF).reshape(ndp * ny, own_in, 3 * chan)
    in_sum = lax.all_to_all(in_sum, GROUP, 0, 0, tiled=True)
    in_sum = in_sum.reshape(ndp, ny, own_in, 3, nz, own_in).transpose(2, 3, 0, 4, 1, 5)
    in_grad = in_sum.reshape(own_in, 3 * width).astype(F32)
    gain_one_grad = jnp.sum(in_grad * in_weight.astype(F32), axis=1) / gain_one.astype(F32)

    input_grad = dh1 + norm_back(da, x, rms_scale(x), gain_a)
    return (
        mixed.reshape(slots, span, width),
        input_grad.reshape(slots, span, width),
        in_grad,
        conv_grad,
        out_grad,
        gain_one_grad,
        gain_two_grad,
        gate_grad,
        up_grad,
        down_grad,
    )


def solution(mesh):
    dp, seq = mesh.shape["dp"], mesh.shape["seq"]
    fine = Mesh(mesh.devices.reshape(dp // 2, 2, seq // 2, 2), ("x", "c", "z", "y"))
    slot, place = ("x", "c"), ("z", "y")
    every = slot + place
    in_specs = (
        P(slot, place, None),
        P(slot, place, None),
        P(slot),
        P(every, None),
        P(None, every),
        P(every, None),
        P(every),
        P(every),
        P(every, None),
        P(every, None),
        P(every, None),
    )
    out_specs = (
        P(slot, place, None),
        P(slot, place, None),
        P(every, None),
        P(None, every),
        P(every, None),
        P(every),
        P(every),
        P(every, None),
        P(every, None),
        P(every, None),
    )
    return jax.shard_map(
        on_device, mesh=fine, in_specs=in_specs, out_specs=out_specs, check_vma=False
    )
```

```python
import jax
import jax.numpy as jnp
from jax import lax
from jax.experimental import pallas as pl
from jax.experimental.pallas import tpu as pltpu
from jax.sharding import Mesh
from jax.sharding import PartitionSpec as P

BF = jnp.bfloat16
F32 = jnp.float32
GROUP = ("x", "c", "y")


def ring_of(count):
    return [0] + list(range(1, count, 2)) + list(range(count - 2 + count % 2, 0, -2))


def send(block, hop, sizes):
    nx, nc, ny = sizes
    dx, dc, dy = hop
    route = []
    for i in range(nx):
        for j in range(nc):
            for k in range(ny):
                source = (i * nc + j) * ny + k
                target = (((i + dx) % nx) * nc + (j + dc) % nc) * ny + (k + dy) % ny
                route.append((source, target))
    return lax.ppermute(block, GROUP, route)


def mirror(hop, sizes):
    return tuple((-h) % n for h, n in zip(hop, sizes))


def fetch(block, hop, sizes):
    return send(block, mirror(hop, sizes), sizes)


def near_gather(block, sizes):
    nx, nc, ny = sizes
    got = {(0, 0): block}
    for dx in range(1, nx):
        got[dx, 0] = fetch(block, (dx, 0, 0), sizes)
    for dy in range(1, ny):
        got[0, dy] = fetch(block, (0, 0, dy), sizes)
    return got


def far_gather(got, sizes):
    nx, nc, ny = sizes
    half = got[0, 0].shape[0] // 2
    got = dict(got)
    for dx in range(1, nx):
        for dy in range(1, ny):
            one = fetch(got[dx, 0][:half], (0, 0, dy), sizes)
            two = fetch(got[0, dy][half:], (dx, 0, 0), sizes)
            got[dx, dy] = jnp.concatenate([one, two], axis=0)
    full = {}
    for (dx, dy), value in got.items():
        full[dx, 0, dy] = value
        for dc in range(1, nc):
            full[dx, dc, dy] = fetch(value, (0, dc, 0), sizes)
    return full


class GroupSum:
    def __init__(self, near, far, sizes):
        nx, _, ny = sizes
        self.sizes = sizes
        self.keys = [(dx, dy) for dx in range(nx) for dy in range(ny)]
        self.here = {key: near[i] for i, key in enumerate(self.keys)}
        self.cross = send(far, (0, 1, 0), sizes)
        self.half = near.shape[1] // 2

    def pair(self, key):
        return self.here[key].astype(F32) + self.cross[self.keys.index(key)].astype(F32)

    def start_far(self):
        half = self.half
        self.more = {}
        for dx, dy in self.keys:
            if dx and dy:
                total = self.pair((dx, dy)).astype(BF)
                self.more[dx, dy] = (
                    send(total[:half], (dx, 0, 0), self.sizes),
                    send(total[half:], (0, 0, dy), self.sizes),
                )

    def start_near(self):
        half = self.half
        self.last = {}
        for key in self.keys:
            if (key[0] == 0) == (key[1] == 0):
                continue
            total = self.pair(key)
            low, high = total[:half], total[half:]
            for (dx, dy), (one, two) in self.more.items():
                if key == (0, dy):
                    low = low + one.astype(F32)
                if key == (dx, 0):
                    high = high + two.astype(F32)
            total = jnp.concatenate([low, high], axis=0).astype(BF)
            self.last[key] = send(total, (key[0], 0, key[1]), self.sizes)

    def terms(self):
        return [self.here[0, 0], self.cross[0]] + list(self.last.values())


class Line:
    def __init__(self, count):
        self.count = count
        self.ring = ring_of(count)
        self.route = [(self.ring[i], self.ring[(i + 1) % count]) for i in range(count)]
        place = {z: i for i, z in enumerate(self.ring)}
        table = [[self.ring[(place[z] - s) % count] for z in range(count)] for s in range(count + 1)]
        here = lax.axis_index("z")
        self.source = [here]
        for s in range(1, count + 1):
            at = jnp.int32(table[s][0])
            for z in range(1, count):
                at = jnp.where(here == z, jnp.int32(table[s][z]), at)
            self.source.append(at)

    def gather(self, block, axis):
        shape = list(block.shape)
        shape.insert(axis, self.count)
        full = jnp.zeros(shape, block.dtype)
        for s in range(self.count):
            if s > 0:
                block = lax.ppermute(block, "z", self.route)
            full = lax.dynamic_update_slice_in_dim(full, jnp.expand_dims(block, axis), self.source[s], axis)
        return full

    def fetch_all(self, block):
        got = [block]
        for s in range(1, self.count):
            route = [(self.ring[i], self.ring[(i + s) % self.count]) for i in range(self.count)]
            got.append(lax.ppermute(block, "z", route))
        return got

    def place(self, blocks, axis):
        shape = list(blocks[0].shape)
        shape.insert(axis, self.count)
        full = jnp.zeros(shape, blocks[0].dtype)
        for s, block in enumerate(blocks):
            full = lax.dynamic_update_slice_in_dim(full, jnp.expand_dims(block, axis), self.source[s], axis)
        return full

    def reduce_direct(self, parts, axis):
        terms = [lax.dynamic_index_in_dim(parts, self.source[0], axis, keepdims=False)]
        for s in range(1, self.count):
            part = lax.dynamic_index_in_dim(parts, self.source[s], axis, keepdims=False)
            route = [(self.ring[i], self.ring[(i - s) % self.count]) for i in range(self.count)]
            terms.append(lax.ppermute(part, "z", route))
        return terms


def dot(left, right):
    return jnp.dot(left, right, preferred_element_type=F32)


def dot_nt(left, right):
    return lax.dot_general(left, right, (((1,), (1,)), ((), ())), preferred_element_type=F32)


def dot_tn(left, right):
    return lax.dot_general(left, right, (((0,), (0,)), ((), ())), preferred_element_type=F32)


def rms_scale(values):
    return lax.rsqrt(jnp.mean(values * values, axis=-1, keepdims=True) + 1e-05)


def norm_back(gradient, values, scale, gain):
    scaled = gradient * gain
    mean_term = jnp.mean(scaled * values, axis=-1, keepdims=True)
    return scale * scaled - values * scale * scale * scale * mean_term


def after(first, second):
    return lax.optimization_barrier((first, second))


def up_to(count, step):
    return (count + step - 1) // step * step


def earlier(values, one, two):
    rows = lax.broadcasted_iota(jnp.int32, values.shape, 0)
    by_one = jnp.where(rows == 0, two, pltpu.roll(values, 1, 0))
    by_two = jnp.where(rows == 0, one, jnp.where(rows == 1, two, pltpu.roll(values, 2, 0)))
    return by_two, by_one


def later(values, one, two):
    count = values.shape[0]
    rows = lax.broadcasted_iota(jnp.int32, values.shape, 0)
    by_one = jnp.where(rows == count - 1, one, pltpu.roll(values, count - 1, 0))
    by_two = jnp.where(
        rows == count - 1, two, jnp.where(rows == count - 2, one, pltpu.roll(values, count - 2, 0))
    )
    return by_one, by_two


def shuffle_plan(ndp, nz, ny):
    return [(dp * ny + y, z) for dp in range(ndp) for z in range(nz) for y in range(ny)]


def cut_body(plan, spots, size, pad, extra, *refs):
    count = 1 + max(which for which, _ in spots)
    sources, more, out = refs[:count], refs[count:-1], refs[-1]
    share = {}
    for at, (group, z) in enumerate(plan):
        share[group, z] = at
    groups = 1 + max(group for group, _ in plan)
    depth = len(plan) // groups
    for group in range(groups):
        for part, (which, start) in enumerate(spots):
            pieces = [
                sources[which][:, start + share[group, z] * size : start + (share[group, z] + 1) * size]
                for z in range(depth)
            ]
            left = pad - depth * size
            if more and part == 0:
                pieces.append(more[0][...])
                left -= extra
            if left:
                pieces.append(jnp.zeros((pieces[0].shape[0], left), pieces[0].dtype))
            out[group, :, part * pad : (part + 1) * pad] = jnp.concatenate(pieces, axis=1)


def cut_columns(sources, size, pad, plan, more=None):
    rows = sources[0].shape[0]
    whole = size * len(plan)
    spots = [(i, start) for i, source in enumerate(sources) for start in range(0, source.shape[1], whole)]
    parts = len(spots)
    groups = 1 + max(group for group, _ in plan)
    extra = 0 if more is None else more.shape[1]
    if rows % 16:
        order = [[i for z in range(len(plan)) for i, p in enumerate(plan) if p == (g, z)] for g in range(groups)]
        out = []
        for group in order:
            row = []
            for part, (which, start) in enumerate(spots):
                pieces = [sources[which][:, start + i * size : start + (i + 1) * size] for i in group]
                left = pad - len(group) * size
                if more is not None and part == 0:
                    pieces.append(more)
                    left -= extra
                pieces.append(jnp.zeros((rows, left), BF))
                row += pieces
            out.append(jnp.concatenate(row, axis=1))
        return jnp.stack(out, axis=0)
    inputs = list(sources) + ([] if more is None else [more])
    return pl.pallas_call(
        lambda *refs: cut_body(plan, spots, size, pad, extra, *refs),
        out_shape=jax.ShapeDtypeStruct((groups, rows, parts * pad), BF),
        compiler_params=pltpu.CompilerParams(vmem_limit_bytes=32 * 2**20),
        cost_estimate=pl.CostEstimate(flops=0, bytes_accessed=6 * 2**20, transcendentals=0),
        name="cut_columns",
    )(*inputs)


def join_body(plan, spots, size, pad, *refs):
    count = 1 + max(which for which, _ in spots)
    shares, weights, gain = refs[0], refs[1 : 1 + count], refs[1 + count]
    grads, gain_grad = refs[2 + count : 2 + 2 * count], refs[-1]
    whole = size * len(plan)
    total = None
    for part, (which, start) in enumerate(spots):
        pieces = [
            shares[group, :, part * pad + z * size : part * pad + (z + 1) * size] for group, z in plan
        ]
        grad = jnp.concatenate(pieces, axis=1).astype(F32)
        grads[which][:, start : start + whole] = grad
        term = jnp.sum(grad * weights[which][:, start : start + whole].astype(F32), axis=1, keepdims=True)
        total = term if total is None else total + term
    gain_grad[...] = total / gain[...]


def join_columns(shares, weights, gain, size, pad, plan):
    rows = weights[0].shape[0]
    whole = size * len(plan)
    spots = [(i, start) for i, weight in enumerate(weights) for start in range(0, weight.shape[1], whole)]
    count = len(weights)
    gain = gain.astype(F32).reshape(rows, 1)
    if rows % 16:
        total, grads = None, [[] for _ in weights]
        for part, (which, start) in enumerate(spots):
            pieces = [shares[g, :, part * pad + z * size : part * pad + (z + 1) * size] for g, z in plan]
            grads[which].append(jnp.concatenate(pieces, axis=1).astype(F32))
            weight = weights[which][:, start : start + whole].astype(F32)
            term = jnp.sum(grads[which][-1] * weight, axis=1, keepdims=True)
            total = term if total is None else total + term
        return [jnp.concatenate(g, axis=1) for g in grads], (total / gain).reshape(rows)
    out = pl.pallas_call(
        lambda *refs: join_body(plan, spots, size, pad, *refs),
        out_shape=[jax.ShapeDtypeStruct(w.shape, F32) for w in weights] + [jax.ShapeDtypeStruct((rows, 1), F32)],
        compiler_params=pltpu.CompilerParams(vmem_limit_bytes=32 * 2**20),
        cost_estimate=pl.CostEstimate(flops=0, bytes_accessed=8 * 2**20, transcendentals=0),
        name="join_columns",
    )(shares, *weights, gain)
    return out[:count], out[count].reshape(rows)


def mix_forward_body(cpad, slots, span, edge, place, x0, x1, e0, e1, w, gain, taps, a, bcx, o_out):
    def normal(ref):
        x = ref[0].astype(F32)
        return (x * rms_scale(x) * gain[...]).astype(BF)

    rows = slots * span
    a0, a1 = normal(x0), normal(x1)
    a[0, 0] = a0
    a[0, 1] = a1
    edges = dot(jnp.concatenate([normal(e0), normal(e1)], axis=0), w[...])
    bcx[0, 2 * rows :] = edges
    past = edges[:edge, :cpad] * edges[:edge, 2 * cpad :]
    low, high = dot(a0, w[...]), dot(a1, w[...])
    bcx[0, :rows] = low
    bcx[0, rows : 2 * rows] = high
    for slot in range(slots):
        both = [part[slot * span : (slot + 1) * span] for part in (low, high)]
        b, c, v = (
            jnp.concatenate([part[:, i * cpad : (i + 1) * cpad] for part in both], axis=0) for i in range(3)
        )
        bx = b * v
        by_two, by_one = earlier(bx, past[2 * slot : 2 * slot + 1], past[2 * slot + 1 : 2 * slot + 2])
        conv = taps[0:1] * by_two + taps[1:2] * by_one + taps[2:3] * bx
        o = (c * conv).astype(BF)
        o_out[0, 0, slot * span : (slot + 1) * span] = o[:span]
        o_out[0, 1, slot * span : (slot + 1) * span] = o[span:]


def mix_forward(x_all, x_past, x_next, w_in, gain, taps, place, sides, slots, span, edge):
    width = x_all.shape[2]
    cpad = w_in.shape[1] // 3
    rows = slots * span
    total = 2 * rows + 2 * edge

    def main(y):
        return pl.BlockSpec((1, rows, width), lambda g, r: (r[2 * g + y], 0, 0))

    rim = pl.BlockSpec((1, edge, width), lambda g, r: (r[2 * g] // 2, 0, 0))

    def fixed(shape):
        return pl.BlockSpec(shape, lambda g, r: (0,) * len(shape))

    return pl.pallas_call(
        lambda *refs: mix_forward_body(cpad, slots, span, edge, *refs),
        grid_spec=pltpu.PrefetchScalarGridSpec(
            num_scalar_prefetch=1,
            grid=(sides,),
            in_specs=[main(0), main(1), rim, rim, fixed(w_in.shape), fixed(gain.shape), fixed(taps.shape)],
            out_specs=[
                pl.BlockSpec((1, 2, rows, width), lambda g, r: (g, 0, 0, 0)),
                pl.BlockSpec((1, total, 3 * cpad), lambda g, r: (g, 0, 0)),
                pl.BlockSpec((1, 2, rows, cpad), lambda g, r: (g, 0, 0, 0)),
            ],
        ),
        out_shape=[
            jax.ShapeDtypeStruct((sides, 2, rows, width), BF),
            jax.ShapeDtypeStruct((sides, total, 3 * cpad), F32),
            jax.ShapeDtypeStruct((sides, 2, rows, cpad), BF),
        ],
        compiler_params=pltpu.CompilerParams(vmem_limit_bytes=56 * 2**20),
        cost_estimate=pl.CostEstimate(
            flops=sides * total * width * 6 * cpad, bytes_accessed=32 * 2**20, transcendentals=0
        ),
        name="mix_forward",
    )(place, x_all, x_all, x_past, x_next, w_in, gain, taps)


def mix_backward_body(
    cpad, slots, span, edge, nat, d0, d1, e1, a, bcx, w, taps, d_part, da_near, da_far, conv_grad, total, grads
):
    step = pl.program_id(0)
    rows = slots * span
    first = step == 0

    @pl.when(first)
    def _():
        conv_grad[...] = jnp.zeros_like(conv_grad)

    edges = bcx[0, 2 * rows :]
    past = edges[:edge, :cpad] * edges[:edge, 2 * cpad :]
    future = e1[0].astype(F32) * edges[edge:, cpad : 2 * cpad]
    sums = [None, None, None]
    for slot in range(slots):
        spots = [slice(y * rows + slot * span, y * rows + (slot + 1) * span) for y in range(2)]
        b, c, v = (
            jnp.concatenate([bcx[0, s, i * cpad : (i + 1) * cpad] for s in spots], axis=0) for i in range(3)
        )
        here = slice(slot * span, (slot + 1) * span)
        d_o = jnp.concatenate([d0[0, here], d1[0, here]], axis=0).astype(F32)
        bx = b * v
        by_two, by_one = earlier(bx, past[2 * slot : 2 * slot + 1], past[2 * slot + 1 : 2 * slot + 2])
        conv = taps[0:1] * by_two + taps[1:2] * by_one + taps[2:3] * bx
        d_c = d_o * conv
        d_conv = d_o * c
        next_one, next_two = later(d_conv, future[2 * slot : 2 * slot + 1], future[2 * slot + 1 : 2 * slot + 2])
        d_bx = taps[2:3] * d_conv + taps[1:2] * next_one + taps[0:1] * next_two
        for i, part in enumerate((d_bx * v, d_c, d_bx * b)):
            part = part.astype(BF)
            grads[spots[0], i * cpad : (i + 1) * cpad] = part[:span]
            grads[spots[1], i * cpad : (i + 1) * cpad] = part[span:]
        for i, term in enumerate((by_two, by_one, bx)):
            term = jnp.sum(d_conv * term, axis=0, keepdims=True)
            sums[i] = term if sums[i] is None else sums[i] + term
    for i in range(3):
        conv_grad[i : i + 1] += sums[i]
    low = dot_nt(grads[:rows], w[...]).astype(BF)
    high = dot_nt(grads[rows:], w[...]).astype(BF)
    even = nat[0] % 2 == 0
    far = step < pl.num_programs(0) // 2

    def keep(ref):
        @pl.when(even)
        def _():
            ref[0, 0] = low
            ref[0, 1] = high

        @pl.when(jnp.logical_not(even))
        def _():
            ref[0, 0] = high
            ref[0, 1] = low

    @pl.when(far)
    def _():
        keep(da_far)

    @pl.when(jnp.logical_not(far))
    def _():
        keep(da_near)

    term = dot_tn(a[...].reshape(2 * rows, a.shape[-1]), grads[...])

    @pl.when(first)
    def _():
        total[...] = term

    @pl.when(jnp.logical_not(first))
    def _():
        total[...] += term

    @pl.when(step == pl.num_programs(0) - 1)
    def _():
        d_part[...] = total[...].astype(BF)


def mix_backward(do_all, do_rim, a_all, bcx, w_in, taps, nat, sides, slots, span, edge):
    width = w_in.shape[0]
    cpad = w_in.shape[1] // 3
    rows = slots * span
    chips = sides // 2

    def side(i, r):
        return r[2 * ((i + chips) % sides)] // 2

    def main(y):
        return pl.BlockSpec((1, rows, cpad), lambda i, r: (2 * side(i, r) + y, 0, 0))

    def fixed(shape):
        return pl.BlockSpec(shape, lambda i, r: (0,) * len(shape))

    da_shape = jax.ShapeDtypeStruct((chips, 2, rows, width), BF)
    work = sides * 2 * rows * width * 3 * cpad * 4
    return pl.pallas_call(
        lambda *refs: mix_backward_body(cpad, slots, span, edge, *refs),
        grid_spec=pltpu.PrefetchScalarGridSpec(
            num_scalar_prefetch=1,
            grid=(sides,),
            in_specs=[
                main(0),
                main(1),
                pl.BlockSpec((1, edge, cpad), lambda i, r: (side(i, r), 0, 0)),
                pl.BlockSpec((1, 2, rows, width), lambda i, r: (side(i, r), 0, 0, 0)),
                pl.BlockSpec((1, 2 * rows + 2 * edge, 3 * cpad), lambda i, r: (side(i, r), 0, 0)),
                fixed(w_in.shape),
                fixed(taps.shape),
            ],
            out_specs=[
                fixed((width, 3 * cpad)),
                pl.BlockSpec((1, 2, rows, width), lambda i, r: (jnp.maximum(i - chips, 0), 0, 0, 0)),
                pl.BlockSpec((1, 2, rows, width), lambda i, r: (jnp.minimum(i, chips - 1), 0, 0, 0)),
                fixed((8, cpad)),
            ],
            scratch_shapes=[pltpu.VMEM((width, 3 * cpad), F32), pltpu.VMEM((2 * rows, 3 * cpad), BF)],
        ),
        out_shape=[
            jax.ShapeDtypeStruct((width, 3 * cpad), BF),
            da_shape,
            da_shape,
            jax.ShapeDtypeStruct((8, cpad), F32),
        ],
        compiler_params=pltpu.CompilerParams(vmem_limit_bytes=60 * 2**20),
        cost_estimate=pl.CostEstimate(flops=work, bytes_accessed=40 * 2**20, transcendentals=0),
        name="mix_backward",
    )(nat, do_all, do_all, do_rim, a_all, bcx, w_in, taps)


def attend_body(count, o, w, x, gain, o_cat, h1, a2):
    joined = jnp.concatenate([o[t] for t in range(count)], axis=1)
    o_cat[...] = joined
    total = x[...].astype(F32) + dot(joined, w[...])
    h1[...] = total
    a2[...] = (total * rms_scale(total) * gain[...]).astype(BF)


def attend(o, w_out, x, gain, block):
    count, rows, cpad = o.shape
    width = w_out.shape[1]

    def row(last):
        return pl.BlockSpec((block, last), lambda i: (i, 0))

    def fixed(shape):
        return pl.BlockSpec(shape, lambda i: (0,) * len(shape))

    return pl.pallas_call(
        lambda *refs: attend_body(count, *refs),
        grid=(rows // block,),
        in_specs=[
            pl.BlockSpec((count, block, cpad), lambda i: (0, i, 0)),
            fixed(w_out.shape),
            row(width),
            fixed(gain.shape),
        ],
        out_specs=[row(count * cpad), row(width), row(width)],
        out_shape=[
            jax.ShapeDtypeStruct((rows, count * cpad), BF),
            jax.ShapeDtypeStruct((rows, width), F32),
            jax.ShapeDtypeStruct((rows, width), BF),
        ],
        compiler_params=pltpu.CompilerParams(vmem_limit_bytes=40 * 2**20),
        cost_estimate=pl.CostEstimate(
            flops=2 * rows * width * count * cpad, bytes_accessed=14 * 2**20, transcendentals=0
        ),
        name="attend",
    )(o, w_out, x, gain)


def turn_body(count, terms, *refs):
    da2 = refs[0][...].astype(F32)
    for ref in refs[1:terms]:
        da2 = da2 + ref[...].astype(F32)
    d_out, h1, gain, w, dh1, datt, d_o = refs[terms:]
    values = h1[...]
    grad = d_out[...].astype(F32) + norm_back(da2, values, rms_scale(values), gain[...])
    dh1[...] = grad
    low = grad.astype(BF)
    datt[...] = low
    cpad = w.shape[0] // count
    for t in range(count):
        d_o[t] = dot_nt(low, w[t * cpad : (t + 1) * cpad]).astype(BF)


def turn(terms, d_out, h1, gain, w_out, count, block):
    rows, width = h1.shape
    cpad = w_out.shape[0] // count

    def row(last):
        return pl.BlockSpec((block, last), lambda i: (i, 0))

    def fixed(shape):
        return pl.BlockSpec(shape, lambda i: (0,) * len(shape))

    return pl.pallas_call(
        lambda *refs: turn_body(count, len(terms), *refs),
        grid=(rows // block,),
        in_specs=[row(width)] * (len(terms) + 2) + [fixed(gain.shape), fixed(w_out.shape)],
        out_specs=[row(width), row(width), pl.BlockSpec((count, block, cpad), lambda i: (0, i, 0))],
        out_shape=[
            jax.ShapeDtypeStruct((rows, width), F32),
            jax.ShapeDtypeStruct((rows, width), BF),
            jax.ShapeDtypeStruct((count, rows, cpad), BF),
        ],
        compiler_params=pltpu.CompilerParams(vmem_limit_bytes=40 * 2**20),
        cost_estimate=pl.CostEstimate(
            flops=2 * rows * width * count * cpad, bytes_accessed=20 * 2**20, transcendentals=0
        ),
        name="turn",
    )(*terms, d_out, h1, gain, w_out)


def finish_body(terms, *refs):
    da = refs[0][...].astype(F32)
    for ref in refs[1:terms]:
        da = da + ref[...].astype(F32)
    x, dh1, gain, out = refs[terms:]
    values = x[...].astype(F32)
    out[...] = dh1[...] + norm_back(da, values, rms_scale(values), gain[...])


def finish(terms, x, dh1, gain, block):
    rows, width = dh1.shape
    spec = pl.BlockSpec((block, width), lambda i: (i, 0))
    return pl.pallas_call(
        lambda *refs: finish_body(len(terms), *refs),
        grid=(rows // block,),
        in_specs=[spec] * (len(terms) + 2) + [pl.BlockSpec(gain.shape, lambda i: (0, 0))],
        out_specs=spec,
        out_shape=jax.ShapeDtypeStruct((rows, width), F32),
        compiler_params=pltpu.CompilerParams(vmem_limit_bytes=40 * 2**20),
        cost_estimate=pl.CostEstimate(flops=rows * width * 8, bytes_accessed=12 * 2**20, transcendentals=0),
        name="finish",
    )(*terms, x, dh1, gain)


def feed_body(hid, hpad, split, a2, d_out, w_both, w_down, m, d_both, f_near, f_far, da_near, da_far):
    gu = dot(a2[0], w_both[...])
    gate, up = gu[:, :hid], gu[:, hpad : hpad + hid]
    dm = dot_nt(d_out[0], w_down[...])
    sigma = 1.0 / (1.0 + jnp.exp(-gate))
    active = gate * sigma
    inner = (active * up).astype(BF)
    m[0] = inner
    if hpad > hid:
        none = jnp.zeros((gu.shape[0], hpad - hid), BF)
        d_both[0, :, hid:hpad] = none
        d_both[0, :, hpad + hid :] = none
    d_both[0, :, :hid] = (dm * up * (sigma * (1.0 + gate * (1.0 - sigma)))).astype(BF)
    d_both[0, :, hpad : hpad + hid] = (dm * active).astype(BF)
    f = dot(inner, w_down[...]).astype(BF)
    da2 = dot_nt(d_both[0], w_both[...]).astype(BF)

    @pl.when(pl.program_id(0) >= split)
    def _():
        f_near[0] = f
        da_near[0] = da2

    @pl.when(pl.program_id(0) < split)
    def _():
        f_far[0] = f
        da_far[0] = da2


def feed(a2_all, d_all, w_both, w_down):
    blocks, rows, width = a2_all.shape
    hid, hpad = w_down.shape[0], w_both.shape[1] // 2
    split = blocks // 2

    def part(last):
        return pl.BlockSpec((1, rows, last), lambda i: ((i + split) % blocks, 0, 0))

    near = pl.BlockSpec((1, rows, width), lambda i: (jnp.maximum(i - split, 0), 0, 0))
    far = pl.BlockSpec((1, rows, width), lambda i: (jnp.minimum(i, split - 1), 0, 0))
    half = jax.ShapeDtypeStruct((split, rows, width), BF)

    def fixed(shape):
        return pl.BlockSpec(shape, lambda i: (0,) * len(shape))

    return pl.pallas_call(
        lambda *refs: feed_body(hid, hpad, split, *refs),
        grid=(blocks,),
        in_specs=[part(width), part(width), fixed(w_both.shape), fixed(w_down.shape)],
        out_specs=[part(hid), part(2 * hpad), near, far, near, far],
        out_shape=[
            jax.ShapeDtypeStruct((blocks, rows, hid), BF),
            jax.ShapeDtypeStruct((blocks, rows, 2 * hpad), BF),
            half,
            half,
            half,
            half,
        ],
        compiler_params=pltpu.CompilerParams(vmem_limit_bytes=60 * 2**20),
        cost_estimate=pl.CostEstimate(
            flops=blocks * rows * width * hid * 12, bytes_accessed=64 * 2**20, transcendentals=blocks * rows * hid
        ),
        name="feed",
    )(a2_all, d_all, w_both, w_down)


def on_device(
    tokens,
    cotangent,
    lengths,
    in_weight,
    conv_weight,
    out_weight,
    gain_one,
    gain_two,
    gate_weight,
    up_weight,
    down_weight,
):
    nx, nc, nz, ny = (lax.axis_size(name) for name in ("x", "c", "z", "y"))
    sizes = (nx, nc, ny)
    ndp = nx * nc
    slots, span, width = tokens.shape
    conv_weight_early = conv_weight
    rows = slots * span
    own_in = in_weight.shape[0]
    own_hid = down_weight.shape[0]
    chan, hid = nz * own_in, nz * own_hid
    cpad, hpad = up_to(chan + 2, 128), up_to(hid, 128)
    edge = up_to(2 * slots, 16)
    hops = [(dx, dc, dy) for dc in range(nc) for dx in range(nx) for dy in range(ny)]
    sides = ndp
    line = Line(nz)
    row_y = lax.axis_index("y")
    here = [lax.axis_index(name) for name in GROUP]
    place = []
    for i in range(nx):
        for j in range(nc):
            for k in range(ny):
                far = [(to + n - at) % n for to, at, n in zip((i, j, k), here, sizes)]
                place.append((far[1] * nx + far[0]) * ny + far[2])
    place = jnp.stack(place).astype(jnp.int32)
    turn_at = []
    for dx, dc, dy in hops:
        at = [(at + far) % n for at, far, n in zip(here, (dx, dc, dy), sizes)]
        turn_at.append((at[0] * nc + at[1]) * ny + at[2])
    nat = jnp.stack(turn_at).astype(jnp.int32)
    first = (lax.axis_index("z") * ny + row_y) * span
    positions = first + jnp.arange(span, dtype=jnp.int32)
    mask = (positions[None, :] < lengths[:, None]).astype(F32).reshape(rows, 1)
    up_route = [(z, z + 1) for z in range(nz - 1)]
    down_route = [(z + 1, z) for z in range(nz - 1)]

    def rim(values, start):
        count, last = values.shape[0], values.shape[-1]
        some = values.reshape(count, slots, span, last)[:, :, start : start + 2].reshape(count, 2 * slots, last)
        return jnp.pad(some, ((0, 0), (0, edge - 2 * slots), (0, 0)))

    x_bf = tokens.reshape(rows, width)
    x = x_bf.astype(F32)
    d_out_bf = (mask * cotangent.reshape(rows, width).astype(F32)).astype(BF)

    plan = shuffle_plan(ndp, nz, ny)
    gains = jnp.stack([gain_one, gain_two], axis=1)
    cut = cut_columns([in_weight], own_in, cpad, plan, gains)
    cut = lax.all_to_all(cut, GROUP, 0, 0, tiled=True).reshape(ndp, ny, own_in, 3 * cpad)
    x_all = near_gather(x_bf, sizes)
    taps_here = jnp.pad(conv_weight.T, ((0, 0), (0, 128 - conv_weight.shape[0])))
    out_here = jnp.concatenate([out_weight, taps_here], axis=1)
    cut = line.fetch_all(cut)

    both = cut_columns([gate_weight, up_weight], own_hid, hpad, plan)
    both = lax.all_to_all(both, GROUP, 0, 0, tiled=True).reshape(ndp, ny * own_in, 2 * hpad)
    x_all, both, out_here = lax.optimization_barrier((x_all, both, out_here))
    w_out = line.fetch_all(out_here)
    w_both = lax.all_gather(both, "z", axis=1, tiled=True).reshape(width, 2 * hpad)

    x_all = far_gather(x_all, sizes)
    x_all = jnp.stack([x_all[h] for h in hops], axis=0)
    pair = x_all.reshape(sides, ny, rows, width)
    even = row_y == 0
    x_past = lax.ppermute(rim(jnp.where(even, pair[:, 1], pair[:, 0]), span - 2), "z", up_route)
    x_next = lax.ppermute(rim(jnp.where(even, pair[:, 0], pair[:, 1]), 0), "z", down_route)
    (x_all, x_past, x_next, w_out), (d_out_bf, down_weight, cut) = after(
        (x_all, x_past, x_next, w_out), (d_out_bf, down_weight, cut)
    )
    w_down = lax.all_gather(down_weight, "z", axis=0, tiled=True)
    w_in = line.place(cut, 1).reshape(width, 3 * cpad)
    gain_a = w_in[:, chan].astype(F32).reshape(1, width)
    gain_b = w_in[:, chan + 1].astype(F32).reshape(1, width)

    w_out = line.place(w_out, 0).reshape(chan, width + 128)
    taps = w_out[:, width : width + 8].astype(F32).T
    taps = jnp.pad(taps, ((0, 0), (0, cpad - chan)))
    w_out = w_out[:, :width]
    w_out = near_gather(w_out, sizes)
    d_all = near_gather(d_out_bf, sizes)

    a_all, bcx, o_all = mix_forward(x_all, x_past, x_next, w_in, gain_a, taps, place, sides, slots, span, edge)
    o_all, w_out = lax.optimization_barrier((o_all, w_out))
    o_own = lax.all_to_all(o_all.reshape(len(hops), rows, cpad), GROUP, 0, 0, tiled=True)
    o_own, d_all = lax.optimization_barrier((o_own, d_all))
    w_some = far_gather(w_out, sizes)
    d_all = far_gather(d_all, sizes)
    w_out = jnp.zeros((len(hops), cpad, width), BF)
    for i, h in enumerate(hops):
        w_out = lax.dynamic_update_slice(w_out, w_some[h][None], (turn_at[i], 0, 0))
    w_out = w_out.reshape(len(hops) * cpad, width)
    block = rows // 2
    o_cat, h1, a2 = attend(o_own, w_out, x_bf, gain_b, block)
    a2, d_all = lax.optimization_barrier((a2, d_all))
    d_all = jnp.stack([d_all[h] for h in hops], axis=0)
    a2_all = far_gather(near_gather(a2, sizes), sizes)
    a2_all = jnp.stack([a2_all[h] for h in hops], axis=0)

    m, d_both, f_near, f_far, da_near, da_far = feed(a2_all, d_all, w_both, w_down)
    hold = lax.optimization_barrier
    da2 = GroupSum(da_near, da_far, sizes)
    d_flat = d_all.reshape(-1, width)
    both_part = dot_tn(a2_all.reshape(-1, width), d_both.reshape(-1, 2 * hpad)).astype(BF)
    both_sum = lax.psum_scatter(
        both_part.reshape(ndp, nz * ny * own_in, 2 * hpad), "z", scatter_dimension=1, tiled=True
    )
    da2.cross, both_part = hold((da2.cross, both_part))
    da2.start_far()
    f = GroupSum(f_near, f_far, sizes)
    down_part = dot_tn(m.reshape(-1, hid), d_flat).astype(BF)
    da2.more, f.cross = hold((da2.more, f.cross))
    da2.start_near()
    da2.last, f.cross, down_part = hold((da2.last, f.cross, down_part))
    down_grad = lax.psum_scatter(down_part, "z", scatter_dimension=0, tiled=True).astype(F32)

    f.start_far()
    dh1, datt, do_own = turn(da2.terms(), d_out_bf, h1, gain_b, w_out, len(hops), block)
    do_all = lax.all_to_all(do_own, GROUP, 0, 0, tiled=True)
    out_part = dot_tn(o_cat, datt).astype(BF).reshape(len(hops), cpad, width)[:, :chan]
    out_near = jnp.stack(
        [lax.dynamic_index_in_dim(out_part, turn_at[i], 0, keepdims=False) for i in range(ndp)], axis=0
    )
    out_far = jnp.stack(
        [lax.dynamic_index_in_dim(out_part, turn_at[i], 0, keepdims=False) for i in range(ndp, 2 * ndp)], axis=0
    )
    out = GroupSum(out_near, out_far, sizes)
    do_all, f.more, out.cross = hold((do_all, f.more, out.cross))
    do_rim = lax.ppermute(rim(do_all.reshape(sides, ny, rows, cpad)[:, 0], 0), "z", down_route)
    do_rim, f.more, out.cross = hold((do_rim, f.more, out.cross))
    f.start_near()
    out.start_far()

    in_part, da_near, da_far, conv_part = mix_backward(
        do_all, do_rim, a_all, bcx, w_in, taps, nat, sides, slots, span, edge
    )
    (in_part, da_near, da_far, conv_part), f.last, out.more = hold(
        ((in_part, da_near, da_far, conv_part), f.last, out.more)
    )
    flat = (ndp, rows, width)
    da = GroupSum(da_near.reshape(flat), da_far.reshape(flat), sizes)
    in_sum = line.reduce_direct(in_part.reshape(ndp, nz, ny, own_in, 3 * cpad), 1)
    both_sum = lax.all_to_all(both_sum.reshape(ndp * ny, own_in, 2 * hpad), GROUP, 0, 0, tiled=True)
    da.cross, both_sum = hold((da.cross, both_sum))
    da.start_far()
    out.start_near()
    da.more, out.last, in_sum[1], in_sum[-1] = hold((da.more, out.last, in_sum[1], in_sum[-1]))
    da.start_near()
    out_sum = sum(term.astype(F32) for term in out.terms()).astype(BF)
    out_grad = line.reduce_direct(out_sum.reshape(nz, own_in, width), 0)
    conv_grad = line.reduce_direct(conv_part[:3, :chan].reshape(3, nz, own_in), 1)
    (gate_grad, up_grad), gain_two_grad = join_columns(
        both_sum, [gate_weight, up_weight], gain_two, own_hid, hpad, plan
    )
    total = h1
    for term in f.terms():
        total = total + term.astype(F32)
    mixed = (mask * total).astype(BF)
    in_sum, da.last, mixed = hold((in_sum, da.last, mixed))
    in_sum = sum(term.astype(F32) for term in in_sum).astype(BF)
    in_sum = lax.all_to_all(in_sum.reshape(ndp * ny, own_in, 3 * cpad), GROUP, 0, 0, tiled=True)
    input_grad = finish(da.terms(), x_bf, dh1, gain_a, block)
    out_grad = sum(term.astype(F32) for term in out_grad)
    conv_grad = sum(conv_grad)
    (in_grad,), gain_one_grad = join_columns(in_sum, [in_weight], gain_one, own_in, cpad, plan)
    return (
        mixed.reshape(slots, span, width),
        input_grad.reshape(slots, span, width),
        in_grad,
        conv_grad,
        out_grad,
        gain_one_grad,
        gain_two_grad,
        gate_grad,
        up_grad,
        down_grad,
    )


def solution(mesh):
    dp, seq = mesh.shape["dp"], mesh.shape["seq"]
    fine = Mesh(mesh.devices.reshape(dp // 2, 2, seq // 2, 2), ("x", "c", "z", "y"))
    slot, place = ("x", "c"), ("z", "y")
    every = slot + place
    in_specs = (
        P(slot, place, None),
        P(slot, place, None),
        P(slot),
        P(every, None),
        P(None, every),
        P(every, None),
        P(every),
        P(every),
        P(every, None),
        P(every, None),
        P(every, None),
    )
    out_specs = (
        P(slot, place, None),
        P(slot, place, None),
        P(every, None),
        P(None, every),
        P(every, None),
        P(every),
        P(every),
        P(every, None),
        P(every, None),
        P(every, None),
    )
    return jax.shard_map(
        on_device, mesh=fine, in_specs=in_specs, out_specs=out_specs, check_vma=False
    )
```

```python
import jax
import jax.numpy as jnp
from jax import lax
from jax.experimental import pallas as pl
from jax.experimental.pallas import tpu as pltpu
from jax.sharding import Mesh
from jax.sharding import PartitionSpec as P

BF = jnp.bfloat16
F32 = jnp.float32
GROUP = ("x", "c", "y")


def ring_of(count):
    return [0] + list(range(1, count, 2)) + list(range(count - 2 + count % 2, 0, -2))


def send(block, hop, sizes):
    nx, nc, ny = sizes
    dx, dc, dy = hop
    route = []
    for i in range(nx):
        for j in range(nc):
            for k in range(ny):
                source = (i * nc + j) * ny + k
                target = (((i + dx) % nx) * nc + (j + dc) % nc) * ny + (k + dy) % ny
                route.append((source, target))
    return lax.ppermute(block, GROUP, route)


def mirror(hop, sizes):
    return tuple((-h) % n for h, n in zip(hop, sizes))


def fetch(block, hop, sizes):
    return send(block, mirror(hop, sizes), sizes)


def near_gather(block, sizes):
    nx, nc, ny = sizes
    got = {(0, 0): block}
    for dx in range(1, nx):
        got[dx, 0] = fetch(block, (dx, 0, 0), sizes)
    for dy in range(1, ny):
        got[0, dy] = fetch(block, (0, 0, dy), sizes)
    return got


def diag_gather(got, sizes):
    nx, _, ny = sizes
    half = got[0, 0].shape[0] // 2
    got = dict(got)
    for dx in range(1, nx):
        for dy in range(1, ny):
            one = fetch(got[dx, 0][:half], (0, 0, dy), sizes)
            two = fetch(got[0, dy][half:], (dx, 0, 0), sizes)
            got[dx, dy] = jnp.concatenate([one, two], axis=0)
    return got


def cross_gather(got, sizes):
    full = {}
    for (dx, dy), value in got.items():
        full[dx, 0, dy] = value
        for dc in range(1, sizes[1]):
            full[dx, dc, dy] = fetch(value, (0, dc, 0), sizes)
    return full


def far_gather(got, sizes):
    return cross_gather(diag_gather(got, sizes), sizes)


def stack(blocks):
    count = len(blocks)

    def body(*refs):
        parts, out, held, came, left = refs[:count], *refs[count:]
        ins = [pltpu.make_async_copy(parts[i], held.at[i], came.at[i]) for i in range(count)]
        outs = [pltpu.make_async_copy(held.at[i], out.at[i], left.at[i]) for i in range(count)]
        for copy in ins:
            copy.start()
        for i in range(count):
            ins[i].wait()
            outs[i].start()
        for copy in outs:
            copy.wait()

    return pl.pallas_call(
        body,
        in_specs=[pl.BlockSpec(memory_space=pl.ANY)] * count,
        out_specs=pl.BlockSpec(memory_space=pl.ANY),
        out_shape=jax.ShapeDtypeStruct((count, *blocks[0].shape), blocks[0].dtype),
        scratch_shapes=[
            pltpu.VMEM((count, *blocks[0].shape), blocks[0].dtype),
            pltpu.SemaphoreType.DMA((count,)),
            pltpu.SemaphoreType.DMA((count,)),
        ],
        compiler_params=pltpu.CompilerParams(vmem_limit_bytes=60 * 2**20),
        cost_estimate=pl.CostEstimate(
            flops=0, bytes_accessed=4 * count * blocks[0].size, transcendentals=0
        ),
        name="stack",
    )(*blocks)


def merge(near, cross, at, one=None, two=None):
    _, rows, width = near.shape
    half = rows // 2
    extra = [] if one is None else [one, two]

    def body(*refs):
        total = refs[0][0].astype(F32) + refs[1][0].astype(F32)
        if extra:
            upper = pl.program_id(0) == 0
            total = total + jnp.where(upper, refs[2][...], refs[3][...]).astype(F32)
        refs[-1][...] = total.astype(BF)

    block = pl.BlockSpec((1, half, width), lambda i: (at, i, 0))
    return pl.pallas_call(
        body,
        grid=(2,),
        in_specs=[block, block] + [pl.BlockSpec((half, width), lambda i: (0, 0))] * len(extra),
        out_specs=pl.BlockSpec((half, width), lambda i: (i, 0)),
        out_shape=jax.ShapeDtypeStruct((rows, width), BF),
        compiler_params=pltpu.CompilerParams(vmem_limit_bytes=24 * 2**20),
        cost_estimate=pl.CostEstimate(flops=3 * rows * width, bytes_accessed=10 * rows * width, transcendentals=0),
        name="merge",
    )(near, cross, *extra)


class GroupSum:
    def __init__(self, near, far, sizes):
        nx, _, ny = sizes
        self.sizes = sizes
        self.keys = [(dx, dy) for dx in range(nx) for dy in range(ny)]
        self.near = near
        self.cross = send(far, (0, 1, 0), sizes)
        self.more, self.last = {}, {}

    def sum_far(self):
        self.total = {
            key: merge(self.near, self.cross, i) for i, key in enumerate(self.keys) if key[0] and key[1]
        }

    def send_far(self):
        for (dx, dy), total in self.total.items():
            half = total.shape[0] // 2
            self.more[dx, dy] = (
                send(total[:half], (dx, 0, 0), self.sizes),
                send(total[half:], (0, 0, dy), self.sizes),
            )

    def sum_near(self):
        self.total = {}
        for i, key in enumerate(self.keys):
            if (key[0] == 0) == (key[1] == 0):
                continue
            low = [one for (dx, dy), (one, _) in self.more.items() if key == (0, dy)]
            high = [two for (dx, dy), (_, two) in self.more.items() if key == (dx, 0)]
            none = jnp.zeros((self.near.shape[1] // 2, self.near.shape[2]), BF)
            low = sum(v.astype(F32) for v in low[1:]) + low[0].astype(F32) if len(low) > 1 else (low + [none])[0]
            high = sum(v.astype(F32) for v in high[1:]) + high[0].astype(F32) if len(high) > 1 else (high + [none])[0]
            self.total[key] = merge(self.near, self.cross, i, low.astype(BF), high.astype(BF))

    def send_near(self):
        for key, total in self.total.items():
            self.last[key] = send(total, (key[0], 0, key[1]), self.sizes)

    def terms(self):
        return [self.near, self.cross] + [v[None] for v in self.last.values()]


class Line:
    def __init__(self, count):
        self.count = count
        self.ring = ring_of(count)
        self.route = [(self.ring[i], self.ring[(i + 1) % count]) for i in range(count)]
        place = {z: i for i, z in enumerate(self.ring)}
        table = [[self.ring[(place[z] - s) % count] for z in range(count)] for s in range(count + 1)]
        here = lax.axis_index("z")
        self.source = [here]
        for s in range(1, count + 1):
            at = jnp.int32(table[s][0])
            for z in range(1, count):
                at = jnp.where(here == z, jnp.int32(table[s][z]), at)
            self.source.append(at)

    def gather(self, block, axis):
        shape = list(block.shape)
        shape.insert(axis, self.count)
        full = jnp.zeros(shape, block.dtype)
        for s in range(self.count):
            if s > 0:
                block = lax.ppermute(block, "z", self.route)
            full = lax.dynamic_update_slice_in_dim(full, jnp.expand_dims(block, axis), self.source[s], axis)
        return full

    def fetch_all(self, block):
        got = [block]
        for s in range(1, self.count):
            route = [(self.ring[i], self.ring[(i + s) % self.count]) for i in range(self.count)]
            got.append(lax.ppermute(block, "z", route))
        return got

    def place(self, blocks, axis):
        shape = list(blocks[0].shape)
        shape.insert(axis, self.count)
        full = jnp.zeros(shape, blocks[0].dtype)
        for s, block in enumerate(blocks):
            full = lax.dynamic_update_slice_in_dim(full, jnp.expand_dims(block, axis), self.source[s], axis)
        return full

    def reduce_direct(self, parts, axis, steps=None):
        terms = [lax.dynamic_index_in_dim(parts, self.source[0], axis, keepdims=False)]
        for s in steps or range(1, self.count):
            part = lax.dynamic_index_in_dim(parts, self.source[s], axis, keepdims=False)
            route = [(self.ring[i], self.ring[(i - s) % self.count]) for i in range(self.count)]
            terms.append(lax.ppermute(part, "z", route))
        return terms


def dot(left, right):
    return jnp.dot(left, right, preferred_element_type=F32)


def dot_nt(left, right):
    return lax.dot_general(left, right, (((1,), (1,)), ((), ())), preferred_element_type=F32)


def dot_tn(left, right):
    return lax.dot_general(left, right, (((0,), (0,)), ((), ())), preferred_element_type=F32)


def rms_scale(values):
    return lax.rsqrt(jnp.mean(values * values, axis=-1, keepdims=True) + 1e-05)


def norm_back(gradient, values, scale, gain):
    scaled = gradient * gain
    mean_term = jnp.mean(scaled * values, axis=-1, keepdims=True)
    return scale * scaled - values * scale * scale * scale * mean_term


def after(first, second):
    return lax.optimization_barrier((first, second))


def up_to(count, step):
    return (count + step - 1) // step * step


def earlier(values, one, two):
    rows = lax.broadcasted_iota(jnp.int32, values.shape, 0)
    by_one = jnp.where(rows == 0, two, pltpu.roll(values, 1, 0))
    by_two = jnp.where(rows == 0, one, jnp.where(rows == 1, two, pltpu.roll(values, 2, 0)))
    return by_two, by_one


def later(values, one, two):
    count = values.shape[0]
    rows = lax.broadcasted_iota(jnp.int32, values.shape, 0)
    by_one = jnp.where(rows == count - 1, one, pltpu.roll(values, count - 1, 0))
    by_two = jnp.where(
        rows == count - 1, two, jnp.where(rows == count - 2, one, pltpu.roll(values, count - 2, 0))
    )
    return by_one, by_two


def shuffle_plan(ndp, nz, ny):
    return [(dp * ny + y, z) for dp in range(ndp) for z in range(nz) for y in range(ny)]


def cut_body(plan, spots, size, pad, extra, *refs):
    count = 1 + max(which for which, _ in spots)
    sources, more, out = refs[:count], refs[count:-1], refs[-1]
    share = {}
    for at, (group, z) in enumerate(plan):
        share[group, z] = at
    groups = 1 + max(group for group, _ in plan)
    depth = len(plan) // groups
    for group in range(groups):
        for part, (which, start) in enumerate(spots):
            pieces = [
                sources[which][:, start + share[group, z] * size : start + (share[group, z] + 1) * size]
                for z in range(depth)
            ]
            left = pad - depth * size
            if more and part == 0:
                pieces.append(more[0][...])
                left -= extra
            if left:
                pieces.append(jnp.zeros((pieces[0].shape[0], left), pieces[0].dtype))
            out[group, :, part * pad : (part + 1) * pad] = jnp.concatenate(pieces, axis=1)


def cut_columns(sources, size, pad, plan, more=None):
    rows = sources[0].shape[0]
    whole = size * len(plan)
    spots = [(i, start) for i, source in enumerate(sources) for start in range(0, source.shape[1], whole)]
    parts = len(spots)
    groups = 1 + max(group for group, _ in plan)
    extra = 0 if more is None else more.shape[1]
    if rows % 16:
        order = [[i for z in range(len(plan)) for i, p in enumerate(plan) if p == (g, z)] for g in range(groups)]
        out = []
        for group in order:
            row = []
            for part, (which, start) in enumerate(spots):
                pieces = [sources[which][:, start + i * size : start + (i + 1) * size] for i in group]
                left = pad - len(group) * size
                if more is not None and part == 0:
                    pieces.append(more)
                    left -= extra
                pieces.append(jnp.zeros((rows, left), BF))
                row += pieces
            out.append(jnp.concatenate(row, axis=1))
        return jnp.stack(out, axis=0)
    inputs = list(sources) + ([] if more is None else [more])
    return pl.pallas_call(
        lambda *refs: cut_body(plan, spots, size, pad, extra, *refs),
        out_shape=jax.ShapeDtypeStruct((groups, rows, parts * pad), BF),
        compiler_params=pltpu.CompilerParams(vmem_limit_bytes=32 * 2**20),
        cost_estimate=pl.CostEstimate(flops=0, bytes_accessed=6 * 2**20, transcendentals=0),
        name="cut_columns",
    )(*inputs)


def join_body(plan, spots, size, pad, *refs):
    count = 1 + max(which for which, _ in spots)
    shares, weights, gain = refs[0], refs[1 : 1 + count], refs[1 + count]
    grads, gain_grad = refs[2 + count : 2 + 2 * count], refs[-1]
    whole = size * len(plan)
    total = None
    for part, (which, start) in enumerate(spots):
        pieces = [
            shares[group, :, part * pad + z * size : part * pad + (z + 1) * size] for group, z in plan
        ]
        grad = jnp.concatenate(pieces, axis=1).astype(F32)
        grads[which][:, start : start + whole] = grad
        term = jnp.sum(grad * weights[which][:, start : start + whole].astype(F32), axis=1, keepdims=True)
        total = term if total is None else total + term
    gain_grad[...] = total / gain[...]


def join_columns(shares, weights, gain, size, pad, plan):
    rows = weights[0].shape[0]
    whole = size * len(plan)
    spots = [(i, start) for i, weight in enumerate(weights) for start in range(0, weight.shape[1], whole)]
    count = len(weights)
    gain = gain.astype(F32).reshape(rows, 1)
    if rows % 16:
        total, grads = None, [[] for _ in weights]
        for part, (which, start) in enumerate(spots):
            pieces = [shares[g, :, part * pad + z * size : part * pad + (z + 1) * size] for g, z in plan]
            grads[which].append(jnp.concatenate(pieces, axis=1).astype(F32))
            weight = weights[which][:, start : start + whole].astype(F32)
            term = jnp.sum(grads[which][-1] * weight, axis=1, keepdims=True)
            total = term if total is None else total + term
        return [jnp.concatenate(g, axis=1) for g in grads], (total / gain).reshape(rows)
    out = pl.pallas_call(
        lambda *refs: join_body(plan, spots, size, pad, *refs),
        out_shape=[jax.ShapeDtypeStruct(w.shape, F32) for w in weights] + [jax.ShapeDtypeStruct((rows, 1), F32)],
        compiler_params=pltpu.CompilerParams(vmem_limit_bytes=32 * 2**20),
        cost_estimate=pl.CostEstimate(flops=0, bytes_accessed=8 * 2**20, transcendentals=0),
        name="join_columns",
    )(shares, *weights, gain)
    return out[:count], out[count].reshape(rows)


def mix_forward_body(cpad, slots, span, edge, place, x0, x1, e0, e1, w, gain, taps, a, bcx, o_out):
    def normal(ref):
        x = ref[0].astype(F32)
        return (x * rms_scale(x) * gain[...]).astype(BF)

    rows = slots * span
    a0, a1 = normal(x0), normal(x1)
    a[0, 0] = a0
    a[0, 1] = a1
    edges = dot(jnp.concatenate([normal(e0), normal(e1)], axis=0), w[...])
    bcx[0, 2 * rows :] = edges
    past = edges[:edge, :cpad] * edges[:edge, 2 * cpad :]
    low, high = dot(a0, w[...]), dot(a1, w[...])
    bcx[0, :rows] = low
    bcx[0, rows : 2 * rows] = high
    for slot in range(slots):
        both = [part[slot * span : (slot + 1) * span] for part in (low, high)]
        b, c, v = (
            jnp.concatenate([part[:, i * cpad : (i + 1) * cpad] for part in both], axis=0) for i in range(3)
        )
        bx = b * v
        by_two, by_one = earlier(bx, past[2 * slot : 2 * slot + 1], past[2 * slot + 1 : 2 * slot + 2])
        conv = taps[0:1] * by_two + taps[1:2] * by_one + taps[2:3] * bx
        o = (c * conv).astype(BF)
        o_out[0, 0, slot * span : (slot + 1) * span] = o[:span]
        o_out[0, 1, slot * span : (slot + 1) * span] = o[span:]


def mix_forward(x_all, w_in, gain, taps, place, sides, slots, span, edge):
    width = x_all.shape[2]
    cpad = w_in.shape[1] // 3
    rows = slots * span
    total = 2 * rows + 2 * edge

    def main(y):
        return pl.BlockSpec((1, rows, width), lambda g, r: (r[2 * g + y], 0, 0))

    def rim(y):
        return pl.BlockSpec((1, edge, width), lambda g, r: (r[2 * g + y], rows // edge, 0))

    def fixed(shape):
        return pl.BlockSpec(shape, lambda g, r: (0,) * len(shape))

    return pl.pallas_call(
        lambda *refs: mix_forward_body(cpad, slots, span, edge, *refs),
        grid_spec=pltpu.PrefetchScalarGridSpec(
            num_scalar_prefetch=1,
            grid=(sides,),
            in_specs=[main(0), main(1), rim(0), rim(1), fixed(w_in.shape), fixed(gain.shape), fixed(taps.shape)],
            out_specs=[
                pl.BlockSpec((1, 2, rows, width), lambda g, r: (g, 0, 0, 0)),
                pl.BlockSpec((1, total, 3 * cpad), lambda g, r: (g, 0, 0)),
                pl.BlockSpec((1, 2, rows, cpad), lambda g, r: (g, 0, 0, 0)),
            ],
        ),
        out_shape=[
            jax.ShapeDtypeStruct((sides, 2, rows, width), BF),
            jax.ShapeDtypeStruct((sides, total, 3 * cpad), F32),
            jax.ShapeDtypeStruct((sides, 2, rows, cpad), BF),
        ],
        compiler_params=pltpu.CompilerParams(vmem_limit_bytes=56 * 2**20),
        cost_estimate=pl.CostEstimate(
            flops=sides * total * width * 6 * cpad, bytes_accessed=32 * 2**20, transcendentals=0
        ),
        name="mix_forward",
    )(place, x_all, x_all, x_all, x_all, w_in, gain, taps)


def mix_backward_body(
    cpad, slots, span, edge, nat, d0, d1, e1, a, bcx, w, taps, d_part, da_near, da_far, conv_grad, total, grads
):
    step = pl.program_id(0)
    rows = slots * span
    first = step == 0

    @pl.when(first)
    def _():
        conv_grad[...] = jnp.zeros_like(conv_grad)

    edges = bcx[0, 2 * rows :]
    past = edges[:edge, :cpad] * edges[:edge, 2 * cpad :]
    future = e1[0].astype(F32) * edges[edge:, cpad : 2 * cpad]
    sums = [None, None, None]
    for slot in range(slots):
        spots = [slice(y * rows + slot * span, y * rows + (slot + 1) * span) for y in range(2)]
        b, c, v = (
            jnp.concatenate([bcx[0, s, i * cpad : (i + 1) * cpad] for s in spots], axis=0) for i in range(3)
        )
        here = slice(slot * span, (slot + 1) * span)
        d_o = jnp.concatenate([d0[0, here], d1[0, here]], axis=0).astype(F32)
        bx = b * v
        by_two, by_one = earlier(bx, past[2 * slot : 2 * slot + 1], past[2 * slot + 1 : 2 * slot + 2])
        conv = taps[0:1] * by_two + taps[1:2] * by_one + taps[2:3] * bx
        d_c = d_o * conv
        d_conv = d_o * c
        next_one, next_two = later(d_conv, future[2 * slot : 2 * slot + 1], future[2 * slot + 1 : 2 * slot + 2])
        d_bx = taps[2:3] * d_conv + taps[1:2] * next_one + taps[0:1] * next_two
        for i, part in enumerate((d_bx * v, d_c, d_bx * b)):
            part = part.astype(BF)
            grads[spots[0], i * cpad : (i + 1) * cpad] = part[:span]
            grads[spots[1], i * cpad : (i + 1) * cpad] = part[span:]
        for i, term in enumerate((by_two, by_one, bx)):
            term = jnp.sum(d_conv * term, axis=0, keepdims=True)
            sums[i] = term if sums[i] is None else sums[i] + term
    for i in range(3):
        conv_grad[i : i + 1] += sums[i]
    low = dot_nt(grads[:rows], w[...]).astype(BF)
    high = dot_nt(grads[rows:], w[...]).astype(BF)
    even = nat[0] % 2 == 0
    far = step < pl.num_programs(0) // 2

    def keep(ref):
        @pl.when(even)
        def _():
            ref[0, 0] = low
            ref[0, 1] = high

        @pl.when(jnp.logical_not(even))
        def _():
            ref[0, 0] = high
            ref[0, 1] = low

    @pl.when(far)
    def _():
        keep(da_far)

    @pl.when(jnp.logical_not(far))
    def _():
        keep(da_near)

    term = dot_tn(a[...].reshape(2 * rows, a.shape[-1]), grads[...])

    @pl.when(first)
    def _():
        total[...] = term

    @pl.when(jnp.logical_not(first))
    def _():
        total[...] += term

    @pl.when(step == pl.num_programs(0) - 1)
    def _():
        d_part[...] = total[...].astype(BF)


def mix_backward(do_all, do_rim, a_all, bcx, w_in, taps, nat, sides, slots, span, edge):
    width = w_in.shape[0]
    cpad = w_in.shape[1] // 3
    rows = slots * span
    chips = sides // 2

    def side(i, r):
        return r[2 * ((i + chips) % sides)] // 2

    def main(y):
        return pl.BlockSpec((1, rows, cpad), lambda i, r: (2 * side(i, r) + y, 0, 0))

    def fixed(shape):
        return pl.BlockSpec(shape, lambda i, r: (0,) * len(shape))

    da_shape = jax.ShapeDtypeStruct((chips, 2, rows, width), BF)
    work = sides * 2 * rows * width * 3 * cpad * 4
    return pl.pallas_call(
        lambda *refs: mix_backward_body(cpad, slots, span, edge, *refs),
        grid_spec=pltpu.PrefetchScalarGridSpec(
            num_scalar_prefetch=1,
            grid=(sides,),
            in_specs=[
                main(0),
                main(1),
                pl.BlockSpec((1, edge, cpad), lambda i, r: (side(i, r), 0, 0)),
                pl.BlockSpec((1, 2, rows, width), lambda i, r: (side(i, r), 0, 0, 0)),
                pl.BlockSpec((1, 2 * rows + 2 * edge, 3 * cpad), lambda i, r: (side(i, r), 0, 0)),
                fixed(w_in.shape),
                fixed(taps.shape),
            ],
            out_specs=[
                fixed((width, 3 * cpad)),
                pl.BlockSpec((1, 2, rows, width), lambda i, r: (jnp.maximum(i - chips, 0), 0, 0, 0)),
                pl.BlockSpec((1, 2, rows, width), lambda i, r: (jnp.minimum(i, chips - 1), 0, 0, 0)),
                fixed((8, cpad)),
            ],
            scratch_shapes=[pltpu.VMEM((width, 3 * cpad), F32), pltpu.VMEM((2 * rows, 3 * cpad), BF)],
        ),
        out_shape=[
            jax.ShapeDtypeStruct((width, 3 * cpad), BF),
            da_shape,
            da_shape,
            jax.ShapeDtypeStruct((8, cpad), F32),
        ],
        compiler_params=pltpu.CompilerParams(vmem_limit_bytes=60 * 2**20),
        cost_estimate=pl.CostEstimate(flops=work, bytes_accessed=40 * 2**20, transcendentals=0),
        name="mix_backward",
    )(nat, do_all, do_all, do_rim, a_all, bcx, w_in, taps)


def attend_body(count, o, w, x, gain, o_cat, h1, a2):
    joined = jnp.concatenate([o[t] for t in range(count)], axis=1)
    o_cat[...] = joined
    total = x[...].astype(F32) + dot(joined, w[...])
    h1[...] = total
    a2[...] = (total * rms_scale(total) * gain[...]).astype(BF)


def attend(o, w_out, x, gain, block):
    count, rows, cpad = o.shape
    width = w_out.shape[1]

    def row(last):
        return pl.BlockSpec((block, last), lambda i: (i, 0))

    def fixed(shape):
        return pl.BlockSpec(shape, lambda i: (0,) * len(shape))

    return pl.pallas_call(
        lambda *refs: attend_body(count, *refs),
        grid=(rows // block,),
        in_specs=[
            pl.BlockSpec((count, block, cpad), lambda i: (0, i, 0)),
            fixed(w_out.shape),
            row(width),
            fixed(gain.shape),
        ],
        out_specs=[row(count * cpad), row(width), row(width)],
        out_shape=[
            jax.ShapeDtypeStruct((rows, count * cpad), BF),
            jax.ShapeDtypeStruct((rows, width), F32),
            jax.ShapeDtypeStruct((rows, width), BF),
        ],
        compiler_params=pltpu.CompilerParams(vmem_limit_bytes=40 * 2**20),
        cost_estimate=pl.CostEstimate(
            flops=2 * rows * width * count * cpad, bytes_accessed=14 * 2**20, transcendentals=0
        ),
        name="attend",
    )(o, w_out, x, gain)


def turn_body(count, terms, *refs):
    da2 = refs[0][0].astype(F32)
    for ref in refs[1:terms]:
        da2 = da2 + ref[0].astype(F32)
    d_out, h1, gain, w, dh1, datt, d_o = refs[terms:]
    values = h1[...]
    grad = d_out[...].astype(F32) + norm_back(da2, values, rms_scale(values), gain[...])
    dh1[...] = grad
    low = grad.astype(BF)
    datt[...] = low
    cpad = w.shape[0] // count
    for t in range(count):
        d_o[t] = dot_nt(low, w[t * cpad : (t + 1) * cpad]).astype(BF)


def turn(terms, d_out, h1, gain, w_out, count, block):
    rows, width = h1.shape
    cpad = w_out.shape[0] // count

    def row(last):
        return pl.BlockSpec((block, last), lambda i: (i, 0))

    def fixed(shape):
        return pl.BlockSpec(shape, lambda i: (0,) * len(shape))

    return pl.pallas_call(
        lambda *refs: turn_body(count, len(terms), *refs),
        grid=(rows // block,),
        in_specs=[pl.BlockSpec((1, block, width), lambda i: (0, i, 0))] * len(terms)
        + [row(width), row(width), fixed(gain.shape), fixed(w_out.shape)],
        out_specs=[row(width), row(width), pl.BlockSpec((count, block, cpad), lambda i: (0, i, 0))],
        out_shape=[
            jax.ShapeDtypeStruct((rows, width), F32),
            jax.ShapeDtypeStruct((rows, width), BF),
            jax.ShapeDtypeStruct((count, rows, cpad), BF),
        ],
        compiler_params=pltpu.CompilerParams(vmem_limit_bytes=40 * 2**20),
        cost_estimate=pl.CostEstimate(
            flops=2 * rows * width * count * cpad, bytes_accessed=20 * 2**20, transcendentals=0
        ),
        name="turn",
    )(*terms, d_out, h1, gain, w_out)


def finish_body(terms, *refs):
    da = refs[0][0].astype(F32)
    for ref in refs[1:terms]:
        da = da + ref[0].astype(F32)
    x, dh1, gain, out = refs[terms:]
    values = x[...].astype(F32)
    out[...] = dh1[...] + norm_back(da, values, rms_scale(values), gain[...])


def finish(terms, x, dh1, gain, block):
    rows, width = dh1.shape
    spec = pl.BlockSpec((block, width), lambda i: (i, 0))
    return pl.pallas_call(
        lambda *refs: finish_body(len(terms), *refs),
        grid=(rows // block,),
        in_specs=[pl.BlockSpec((1, block, width), lambda i: (0, i, 0))] * len(terms)
        + [spec] * 2
        + [pl.BlockSpec(gain.shape, lambda i: (0, 0))],
        out_specs=spec,
        out_shape=jax.ShapeDtypeStruct((rows, width), F32),
        compiler_params=pltpu.CompilerParams(vmem_limit_bytes=40 * 2**20),
        cost_estimate=pl.CostEstimate(flops=rows * width * 8, bytes_accessed=12 * 2**20, transcendentals=0),
        name="finish",
    )(*terms, x, dh1, gain)


def feed_body(hid, hpad, a2, d_out, w_both, w_down, *refs):
    m, d_both, f, da2 = refs[-4:]
    gu = dot(a2[0], w_both[...])
    gate, up = gu[:, :hid], gu[:, hpad : hpad + hid]
    dm = dot_nt(d_out[0], w_down[...])
    sigma = 1.0 / (1.0 + jnp.exp(-gate))
    active = gate * sigma
    inner = (active * up).astype(BF)
    m[0] = inner
    if hpad > hid:
        none = jnp.zeros((gu.shape[0], hpad - hid), BF)
        d_both[0, :, hid:hpad] = none
        d_both[0, :, hpad + hid :] = none
    d_both[0, :, :hid] = (dm * up * (sigma * (1.0 + gate * (1.0 - sigma)))).astype(BF)
    d_both[0, :, hpad : hpad + hid] = (dm * active).astype(BF)
    f[0] = dot(inner, w_down[...]).astype(BF)
    da2[0] = dot_nt(d_both[0], w_both[...]).astype(BF)


def feed(a2_all, d_all, w_both, w_down, first, kept=()):
    blocks, rows, width = a2_all.shape
    half = blocks // 2
    hid, hpad = w_down.shape[0], w_both.shape[1] // 2

    def part(last):
        return pl.BlockSpec((1, rows, last), lambda i: (i + first, 0, 0))

    def fixed(shape):
        return pl.BlockSpec(shape, lambda i: (0,) * len(shape), pipeline_mode=pl.Buffered(1))

    own = pl.BlockSpec((1, rows, width), lambda i: (i, 0, 0))
    return pl.pallas_call(
        lambda *refs: feed_body(hid, hpad, *refs),
        grid=(half,),
        in_specs=[part(width), part(width), fixed(w_both.shape), fixed(w_down.shape)]
        + [pl.BlockSpec(memory_space=pl.ANY)] * len(kept),
        out_specs=[part(hid), part(2 * hpad), own, own],
        out_shape=[
            jax.ShapeDtypeStruct((blocks, rows, hid), BF),
            jax.ShapeDtypeStruct((blocks, rows, 2 * hpad), BF),
            jax.ShapeDtypeStruct((half, rows, width), BF),
            jax.ShapeDtypeStruct((half, rows, width), BF),
        ],
        input_output_aliases={4 + i: i for i in range(len(kept))},
        compiler_params=pltpu.CompilerParams(vmem_limit_bytes=60 * 2**20),
        cost_estimate=pl.CostEstimate(
            flops=half * rows * width * hid * 12, bytes_accessed=40 * 2**20, transcendentals=half * rows * hid
        ),
        name="feed",
    )(a2_all, d_all, w_both, w_down, *kept)


def on_device(
    tokens,
    cotangent,
    lengths,
    in_weight,
    conv_weight,
    out_weight,
    gain_one,
    gain_two,
    gate_weight,
    up_weight,
    down_weight,
):
    nx, nc, nz, ny = (lax.axis_size(name) for name in ("x", "c", "z", "y"))
    sizes = (nx, nc, ny)
    ndp = nx * nc
    slots, span, width = tokens.shape
    conv_weight_early = conv_weight
    rows = slots * span
    own_in = in_weight.shape[0]
    own_hid = down_weight.shape[0]
    chan, hid = nz * own_in, nz * own_hid
    cpad, hpad = up_to(chan + 2, 128), up_to(hid, 128)
    edge = up_to(2 * slots, 16)
    hops = [(dx, dc, dy) for dc in range(nc) for dx in range(nx) for dy in range(ny)]
    sides = ndp
    line = Line(nz)
    row_y = lax.axis_index("y")
    here = [lax.axis_index(name) for name in GROUP]
    place = []
    for i in range(nx):
        for j in range(nc):
            for k in range(ny):
                far = [(to + n - at) % n for to, at, n in zip((i, j, k), here, sizes)]
                place.append((far[1] * nx + far[0]) * ny + far[2])
    place = jnp.stack(place).astype(jnp.int32)
    turn_at = []
    for dx, dc, dy in hops:
        at = [(at + far) % n for at, far, n in zip(here, (dx, dc, dy), sizes)]
        turn_at.append((at[0] * nc + at[1]) * ny + at[2])
    nat = jnp.stack(turn_at).astype(jnp.int32)
    first = (lax.axis_index("z") * ny + row_y) * span
    positions = first + jnp.arange(span, dtype=jnp.int32)
    mask = (positions[None, :] < lengths[:, None]).astype(F32).reshape(rows, 1)
    rim_route = []
    for z in range(nz - 1):
        rim_route += [(z * ny + 1, (z + 1) * ny), ((z + 1) * ny, z * ny + 1)]
    down_route = [(z + 1, z) for z in range(nz - 1)]

    def rim(values, start):
        count, last = values.shape[0], values.shape[-1]
        some = values.reshape(count, slots, span, last)[:, :, start : start + 2].reshape(count, 2 * slots, last)
        return jnp.pad(some, ((0, 0), (0, edge - 2 * slots), (0, 0)))

    x_bf = tokens.reshape(rows, width)
    x = x_bf.astype(F32)
    d_out_bf = (mask * cotangent.reshape(rows, width).astype(F32)).astype(BF)

    hold = lax.optimization_barrier
    plan = shuffle_plan(ndp, nz, ny)

    gains = jnp.stack([gain_one, gain_two], axis=1)
    cut = cut_columns([in_weight], own_in, cpad, plan, gains)
    cut = lax.all_to_all(cut, GROUP, 0, 0, tiled=True).reshape(ndp, ny, own_in, 3 * cpad)
    taps_here = jnp.pad(conv_weight.T, ((0, 0), (0, 128 - conv_weight.shape[0])))
    w_out = line.fetch_all(jnp.concatenate([out_weight, taps_here], axis=1))
    pairs = tokens.reshape(slots, span, width)
    pairs = jnp.where(row_y == 0, pairs[:, :2], pairs[:, -2:]).reshape(2 * slots, width)
    x_rim = lax.ppermute(jnp.pad(pairs, ((0, edge - 2 * slots), (0, 0))), ("z", "y"), rim_route)
    (cut, w_out, x_rim), (x_late, gate_late) = after((cut, w_out, x_rim), (x_bf, gate_weight))
    x_late = jnp.concatenate([x_late, x_rim], axis=0)

    w_in = lax.all_gather(cut.reshape(ndp, ny * own_in, 3 * cpad), "z", axis=1, tiled=True).reshape(width, 3 * cpad)
    w_out = line.place(w_out, 0).reshape(chan, width + 128)
    taps = w_out[:, width : width + 8].astype(F32).T
    taps = jnp.pad(taps, ((0, 0), (0, cpad - chan)))
    w_out = near_gather(w_out[:, :width], sizes)
    x_all = near_gather(x_late, sizes)
    both = cut_columns([gate_late, up_weight], own_hid, hpad, plan)
    both = lax.all_to_all(both, GROUP, 0, 0, tiled=True).reshape(ndp, ny * own_in, 2 * hpad)
    x_all, both, w_in, w_out = hold((x_all, both, w_in, w_out))

    w_both = lax.all_gather(both, "z", axis=1, tiled=True).reshape(width, 2 * hpad)
    x_all = far_gather(x_all, sizes)
    gain_a = w_in[:, chan].astype(F32).reshape(1, width)
    gain_b = w_in[:, chan + 1].astype(F32).reshape(1, width)
    x_all, (w_out, d_late) = after(x_all, (w_out, d_out_bf))

    w_out = diag_gather(w_out, sizes)
    x_all = stack([x_all[h] for h in hops])
    d_all = near_gather(d_late, sizes)
    a_all, bcx, o_all = mix_forward(x_all, w_in, gain_a, taps, place, sides, slots, span, edge)
    o_all, w_out, d_all = hold((o_all, w_out, d_all))

    o_own = lax.all_to_all(o_all.reshape(len(hops), rows, cpad), GROUP, 0, 0, tiled=True)
    w_some = cross_gather(w_out, sizes)
    d_all = diag_gather(d_all, sizes)
    w_out = jnp.zeros((len(hops), cpad, width), BF)
    for i, h in enumerate(hops):
        w_out = lax.dynamic_update_slice(w_out, w_some[h][None], (turn_at[i], 0, 0))
    w_out = w_out.reshape(len(hops) * cpad, width)
    o_own, w_out = hold((o_own, w_out))

    block = rows // 2
    o_cat, h1, a2 = attend(o_own, w_out, x_bf, gain_b, block)
    (a2, d_all, w_both), down_weight = after((a2, d_all, w_both), down_weight)

    w_down = lax.all_gather(down_weight, "z", axis=0, tiled=True)
    d_all = cross_gather(d_all, sizes)
    a2_all = near_gather(a2, sizes)
    a2_all, d_all = hold((a2_all, d_all))
    d_all = stack([d_all[h] for h in hops])
    a2_all, d_all = hold((diag_gather(a2_all, sizes), d_all))
    a2_all = cross_gather(a2_all, sizes)
    a2_all = stack([a2_all[h] for h in hops])

    m, d_both, f_far, da_far = feed(a2_all, d_all, w_both, w_down, len(hops) // 2)
    m, d_both, f_near, da_near = feed(a2_all, d_all, w_both, w_down, 0, (m, d_both))
    da2 = GroupSum(da_near, da_far, sizes)
    f = GroupSum(f_near, f_far, sizes)
    d_flat = d_all.reshape(-1, width)
    da2.sum_far()
    da2.total, m = after(da2.total, m)
    da2.send_far()
    down_part = dot_tn(m.reshape(-1, hid), d_flat).astype(BF)
    da2.more, f.cross, down_part = hold((da2.more, f.cross, down_part))

    da2.sum_near()
    da2.total, d_both = after(da2.total, d_both)
    da2.send_near()
    both_part = dot_tn(a2_all.reshape(-1, width), d_both.reshape(-1, 2 * hpad)).astype(BF)
    da2.last, both_part, f.cross = hold((da2.last, both_part, f.cross))
    both_sum = lax.psum_scatter(
        both_part.reshape(ndp, nz * ny * own_in, 2 * hpad), "z", scatter_dimension=1, tiled=True
    )

    f.sum_far()
    da2.last, f.total = hold((da2.last, f.total))
    f.send_far()
    dh1, datt, do_own = turn(da2.terms(), d_out_bf, h1, gain_b, w_out, len(hops), block)
    do_own, datt, f.more = hold((do_own, datt, f.more))

    do_all = lax.all_to_all(do_own, GROUP, 0, 0, tiled=True)
    out_part = dot_tn(o_cat, datt).astype(BF).reshape(len(hops), cpad, width)[:, :chan]
    out_near = jnp.stack([lax.dynamic_index_in_dim(out_part, t, 0, keepdims=False) for t in turn_at[:ndp]], axis=0)
    out_far = jnp.stack([lax.dynamic_index_in_dim(out_part, t, 0, keepdims=False) for t in turn_at[ndp:]], axis=0)
    out = GroupSum(out_near, out_far, sizes)
    f.sum_near()
    do_all, out.cross, f.total = hold((do_all, out.cross, f.total))

    do_rim = lax.ppermute(rim(do_all.reshape(sides, ny, rows, cpad)[:, 0], 0), "z", down_route)
    out.sum_far()
    do_rim, f.total, out.total = hold((do_rim, f.total, out.total))

    f.send_near()
    out.send_far()
    in_part, da_near, da_far, conv_part = mix_backward(
        do_all, do_rim, a_all, bcx, w_in, taps, nat, sides, slots, span, edge
    )
    (in_part, da_near, da_far, conv_part), f.last, out.more = hold(
        ((in_part, da_near, da_far, conv_part), f.last, out.more)
    )

    flat = (ndp, rows, width)
    da = GroupSum(da_near.reshape(flat), da_far.reshape(flat), sizes)
    in_part, both_sum = hold((in_part, both_sum))
    in_sum = lax.psum_scatter(
        in_part.reshape(ndp, nz * ny * own_in, 3 * cpad), "z", scatter_dimension=1, tiled=True
    )
    both_sum = lax.all_to_all(both_sum.reshape(ndp * ny, own_in, 2 * hpad), GROUP, 0, 0, tiled=True)
    da.cross = hold(da.cross)

    da.sum_far()
    da.send_far()
    out.sum_near()
    out.send_near()
    da.more, both_sum, out.last = hold((da.more, both_sum, out.last))
    da.sum_near()
    da.total, in_sum = after(da.total, in_sum)
    in_sum, down_part = after(in_sum, down_part)
    down_grad = lax.psum_scatter(down_part, "z", scatter_dimension=0, tiled=True)
    da.send_near()
    in_sum = lax.all_to_all(in_sum.reshape(ndp * ny, own_in, 3 * cpad), GROUP, 0, 0, tiled=True)
    out_sum = sum(term[0].astype(F32) for term in out.terms()).astype(BF)
    out_grad = line.reduce_direct(out_sum.reshape(nz, own_in, width), 0)
    conv_grad = line.reduce_direct(conv_part[:3, :chan].reshape(3, nz, own_in), 1)
    total = h1
    for term in f.terms():
        total = total + term[0].astype(F32)
    mixed = (mask * total).astype(BF)
    (gate_grad, up_grad), gain_two_grad = join_columns(
        both_sum, [gate_weight, up_weight], gain_two, own_hid, hpad, plan
    )
    in_sum, da.last, out_grad, conv_grad, mixed, gate_grad, up_grad = hold(
        (in_sum, da.last, out_grad, conv_grad, mixed, gate_grad, up_grad)
    )

    input_grad = finish(da.terms(), x_bf, dh1, gain_a, block)
    out_grad = sum(term.astype(F32) for term in out_grad)
    conv_grad = sum(conv_grad)
    (in_grad,), gain_one_grad = join_columns(in_sum, [in_weight], gain_one, own_in, cpad, plan)
    down_grad = down_grad.astype(F32)
    return (
        mixed.reshape(slots, span, width),
        input_grad.reshape(slots, span, width),
        in_grad,
        conv_grad,
        out_grad,
        gain_one_grad,
        gain_two_grad,
        gate_grad,
        up_grad,
        down_grad,
    )


def solution(mesh):
    dp, seq = mesh.shape["dp"], mesh.shape["seq"]
    fine = Mesh(mesh.devices.reshape(dp // 2, 2, seq // 2, 2), ("x", "c", "z", "y"))
    slot, place = ("x", "c"), ("z", "y")
    every = slot + place
    in_specs = (
        P(slot, place, None),
        P(slot, place, None),
        P(slot),
        P(every, None),
        P(None, every),
        P(every, None),
        P(every),
        P(every),
        P(every, None),
        P(every, None),
        P(every, None),
    )
    out_specs = (
        P(slot, place, None),
        P(slot, place, None),
        P(every, None),
        P(None, every),
        P(every, None),
        P(every),
        P(every),
        P(every, None),
        P(every, None),
        P(every, None),
    )
    return jax.shard_map(
        on_device, mesh=fine, in_specs=in_specs, out_specs=out_specs, check_vma=False
    )
```

```python
import jax
import jax.numpy as jnp
from jax import lax
from jax.experimental import pallas as pl
from jax.experimental.pallas import tpu as pltpu
from jax.sharding import Mesh
from jax.sharding import PartitionSpec as P

BF = jnp.bfloat16
F32 = jnp.float32
GROUP = ("x", "c", "y")


def ring_of(count):
    return [0] + list(range(1, count, 2)) + list(range(count - 2 + count % 2, 0, -2))


def send(block, hop, sizes):
    nx, nc, ny = sizes
    dx, dc, dy = hop
    route = []
    for i in range(nx):
        for j in range(nc):
            for k in range(ny):
                source = (i * nc + j) * ny + k
                target = (((i + dx) % nx) * nc + (j + dc) % nc) * ny + (k + dy) % ny
                route.append((source, target))
    return lax.ppermute(block, GROUP, route)


def mirror(hop, sizes):
    return tuple((-h) % n for h, n in zip(hop, sizes))


def fetch(block, hop, sizes):
    return send(block, mirror(hop, sizes), sizes)


def near_gather(block, sizes):
    nx, nc, ny = sizes
    got = {(0, 0): block}
    for dx in range(1, nx):
        got[dx, 0] = fetch(block, (dx, 0, 0), sizes)
    for dy in range(1, ny):
        got[0, dy] = fetch(block, (0, 0, dy), sizes)
    return got


def diag_gather(got, sizes):
    nx, _, ny = sizes
    half = got[0, 0].shape[0] // 2
    got = dict(got)
    for dx in range(1, nx):
        for dy in range(1, ny):
            one = fetch(got[dx, 0][:half], (0, 0, dy), sizes)
            two = fetch(got[0, dy][half:], (dx, 0, 0), sizes)
            got[dx, dy] = jnp.concatenate([one, two], axis=0)
    return got


def cross_gather(got, sizes):
    full = {}
    for (dx, dy), value in got.items():
        full[dx, 0, dy] = value
        for dc in range(1, sizes[1]):
            full[dx, dc, dy] = fetch(value, (0, dc, 0), sizes)
    return full


def far_gather(got, sizes):
    return cross_gather(diag_gather(got, sizes), sizes)


def stack(blocks, count=None, first=0, kept=None):
    here = len(blocks)
    count = count or here
    more = [] if kept is None else [kept]

    def body(*refs):
        parts, (out, held, came, left) = refs[:here], refs[-4:]
        ins = [pltpu.make_async_copy(parts[i], held.at[i], came.at[i]) for i in range(here)]
        outs = [pltpu.make_async_copy(held.at[i], out.at[first + i], left.at[i]) for i in range(here)]
        for copy in ins:
            copy.start()
        for i in range(here):
            ins[i].wait()
            outs[i].start()
        for copy in outs:
            copy.wait()

    return pl.pallas_call(
        body,
        in_specs=[pl.BlockSpec(memory_space=pl.ANY)] * (here + len(more)),
        out_specs=pl.BlockSpec(memory_space=pl.ANY),
        out_shape=jax.ShapeDtypeStruct((count, *blocks[0].shape), blocks[0].dtype),
        input_output_aliases={here: 0} if more else {},
        scratch_shapes=[
            pltpu.VMEM((here, *blocks[0].shape), blocks[0].dtype),
            pltpu.SemaphoreType.DMA((here,)),
            pltpu.SemaphoreType.DMA((here,)),
        ],
        compiler_params=pltpu.CompilerParams(vmem_limit_bytes=60 * 2**20),
        cost_estimate=pl.CostEstimate(flops=0, bytes_accessed=4 * here * blocks[0].size, transcendentals=0),
        name="stack",
    )(*blocks, *more)


def merge(near, cross, at, one=None, two=None):
    _, rows, width = near.shape
    half = rows // 2
    extra = [] if one is None else [one, two]

    def body(*refs):
        total = refs[0][0].astype(F32) + refs[1][0].astype(F32)
        if extra:
            upper = pl.program_id(0) == 0
            total = total + jnp.where(upper, refs[2][...], refs[3][...]).astype(F32)
        refs[-1][...] = total.astype(BF)

    block = pl.BlockSpec((1, half, width), lambda i: (at, i, 0))
    return pl.pallas_call(
        body,
        grid=(2,),
        in_specs=[block, block] + [pl.BlockSpec((half, width), lambda i: (0, 0))] * len(extra),
        out_specs=pl.BlockSpec((half, width), lambda i: (i, 0)),
        out_shape=jax.ShapeDtypeStruct((rows, width), BF),
        compiler_params=pltpu.CompilerParams(vmem_limit_bytes=24 * 2**20),
        cost_estimate=pl.CostEstimate(flops=3 * rows * width, bytes_accessed=10 * rows * width, transcendentals=0),
        name="merge",
    )(near, cross, *extra)


class GroupSum:
    def __init__(self, near, far, sizes):
        nx, _, ny = sizes
        self.sizes = sizes
        self.keys = [(dx, dy) for dx in range(nx) for dy in range(ny)]
        self.near = near
        self.cross = send(far, (0, 1, 0), sizes)
        self.more, self.last = {}, {}

    def sum_far(self):
        self.total = {
            key: merge(self.near, self.cross, i) for i, key in enumerate(self.keys) if key[0] and key[1]
        }

    def send_far(self):
        for (dx, dy), total in self.total.items():
            half = total.shape[0] // 2
            self.more[dx, dy] = (
                send(total[:half], (dx, 0, 0), self.sizes),
                send(total[half:], (0, 0, dy), self.sizes),
            )

    def sum_near(self):
        self.total = {}
        for i, key in enumerate(self.keys):
            if (key[0] == 0) == (key[1] == 0):
                continue
            low = [one for (dx, dy), (one, _) in self.more.items() if key == (0, dy)]
            high = [two for (dx, dy), (_, two) in self.more.items() if key == (dx, 0)]
            none = jnp.zeros((self.near.shape[1] // 2, self.near.shape[2]), BF)
            low = sum(v.astype(F32) for v in low[1:]) + low[0].astype(F32) if len(low) > 1 else (low + [none])[0]
            high = sum(v.astype(F32) for v in high[1:]) + high[0].astype(F32) if len(high) > 1 else (high + [none])[0]
            self.total[key] = merge(self.near, self.cross, i, low.astype(BF), high.astype(BF))

    def send_near(self):
        for key, total in self.total.items():
            self.last[key] = send(total, (key[0], 0, key[1]), self.sizes)

    def terms(self):
        return [self.near, self.cross] + [v[None] for v in self.last.values()]


class Line:
    def __init__(self, count):
        self.count = count
        self.ring = ring_of(count)
        self.route = [(self.ring[i], self.ring[(i + 1) % count]) for i in range(count)]
        place = {z: i for i, z in enumerate(self.ring)}
        table = [[self.ring[(place[z] - s) % count] for z in range(count)] for s in range(count + 1)]
        here = lax.axis_index("z")
        self.source = [here]
        for s in range(1, count + 1):
            at = jnp.int32(table[s][0])
            for z in range(1, count):
                at = jnp.where(here == z, jnp.int32(table[s][z]), at)
            self.source.append(at)

    def gather(self, block, axis):
        shape = list(block.shape)
        shape.insert(axis, self.count)
        full = jnp.zeros(shape, block.dtype)
        for s in range(self.count):
            if s > 0:
                block = lax.ppermute(block, "z", self.route)
            full = lax.dynamic_update_slice_in_dim(full, jnp.expand_dims(block, axis), self.source[s], axis)
        return full

    def fetch_all(self, block):
        got = [block]
        for s in range(1, self.count):
            route = [(self.ring[i], self.ring[(i + s) % self.count]) for i in range(self.count)]
            got.append(lax.ppermute(block, "z", route))
        return got

    def place(self, blocks, axis):
        shape = list(blocks[0].shape)
        shape.insert(axis, self.count)
        full = jnp.zeros(shape, blocks[0].dtype)
        for s, block in enumerate(blocks):
            full = lax.dynamic_update_slice_in_dim(full, jnp.expand_dims(block, axis), self.source[s], axis)
        return full

    def reduce_direct(self, parts, axis, steps=None):
        terms = [lax.dynamic_index_in_dim(parts, self.source[0], axis, keepdims=False)]
        for s in steps or range(1, self.count):
            part = lax.dynamic_index_in_dim(parts, self.source[s], axis, keepdims=False)
            route = [(self.ring[i], self.ring[(i - s) % self.count]) for i in range(self.count)]
            terms.append(lax.ppermute(part, "z", route))
        return terms


def dot(left, right):
    return jnp.dot(left, right, preferred_element_type=F32)


def dot_nt(left, right):
    return lax.dot_general(left, right, (((1,), (1,)), ((), ())), preferred_element_type=F32)


def dot_tn(left, right):
    return lax.dot_general(left, right, (((0,), (0,)), ((), ())), preferred_element_type=F32)


def rms_scale(values):
    return lax.rsqrt(jnp.mean(values * values, axis=-1, keepdims=True) + 1e-05)


def norm_back(gradient, values, scale, gain):
    scaled = gradient * gain
    mean_term = jnp.mean(scaled * values, axis=-1, keepdims=True)
    return scale * scaled - values * scale * scale * scale * mean_term


def after(first, second):
    return lax.optimization_barrier((first, second))


def up_to(count, step):
    return (count + step - 1) // step * step


def earlier(values, one, two):
    rows = lax.broadcasted_iota(jnp.int32, values.shape, 0)
    by_one = jnp.where(rows == 0, two, pltpu.roll(values, 1, 0))
    by_two = jnp.where(rows == 0, one, jnp.where(rows == 1, two, pltpu.roll(values, 2, 0)))
    return by_two, by_one


def later(values, one, two):
    count = values.shape[0]
    rows = lax.broadcasted_iota(jnp.int32, values.shape, 0)
    by_one = jnp.where(rows == count - 1, one, pltpu.roll(values, count - 1, 0))
    by_two = jnp.where(
        rows == count - 1, two, jnp.where(rows == count - 2, one, pltpu.roll(values, count - 2, 0))
    )
    return by_one, by_two


def shuffle_plan(ndp, nz, ny):
    return [(dp * ny + y, z) for dp in range(ndp) for z in range(nz) for y in range(ny)]


def cut_body(plan, spots, size, pad, extra, *refs):
    count = 1 + max(which for which, _ in spots)
    sources, more, out = refs[:count], refs[count:-1], refs[-1]
    share = {}
    for at, (group, z) in enumerate(plan):
        share[group, z] = at
    groups = 1 + max(group for group, _ in plan)
    depth = len(plan) // groups
    for group in range(groups):
        for part, (which, start) in enumerate(spots):
            pieces = [
                sources[which][:, start + share[group, z] * size : start + (share[group, z] + 1) * size]
                for z in range(depth)
            ]
            left = pad - depth * size
            if more and part == 0:
                pieces.append(more[0][...])
                left -= extra
            if left:
                pieces.append(jnp.zeros((pieces[0].shape[0], left), pieces[0].dtype))
            out[group, :, part * pad : (part + 1) * pad] = jnp.concatenate(pieces, axis=1)


def cut_columns(sources, size, pad, plan, more=None):
    rows = sources[0].shape[0]
    whole = size * len(plan)
    spots = [(i, start) for i, source in enumerate(sources) for start in range(0, source.shape[1], whole)]
    parts = len(spots)
    groups = 1 + max(group for group, _ in plan)
    extra = 0 if more is None else more.shape[1]
    if rows % 16:
        order = [[i for z in range(len(plan)) for i, p in enumerate(plan) if p == (g, z)] for g in range(groups)]
        out = []
        for group in order:
            row = []
            for part, (which, start) in enumerate(spots):
                pieces = [sources[which][:, start + i * size : start + (i + 1) * size] for i in group]
                left = pad - len(group) * size
                if more is not None and part == 0:
                    pieces.append(more)
                    left -= extra
                pieces.append(jnp.zeros((rows, left), BF))
                row += pieces
            out.append(jnp.concatenate(row, axis=1))
        return jnp.stack(out, axis=0)
    inputs = list(sources) + ([] if more is None else [more])
    return pl.pallas_call(
        lambda *refs: cut_body(plan, spots, size, pad, extra, *refs),
        out_shape=jax.ShapeDtypeStruct((groups, rows, parts * pad), BF),
        compiler_params=pltpu.CompilerParams(vmem_limit_bytes=32 * 2**20),
        cost_estimate=pl.CostEstimate(flops=0, bytes_accessed=6 * 2**20, transcendentals=0),
        name="cut_columns",
    )(*inputs)


def join_body(plan, spots, size, pad, *refs):
    count = 1 + max(which for which, _ in spots)
    shares, weights, gain = refs[0], refs[1 : 1 + count], refs[1 + count]
    grads, gain_grad = refs[2 + count : 2 + 2 * count], refs[-1]
    whole = size * len(plan)
    total = None
    for part, (which, start) in enumerate(spots):
        pieces = [
            shares[group, :, part * pad + z * size : part * pad + (z + 1) * size] for group, z in plan
        ]
        grad = jnp.concatenate(pieces, axis=1).astype(F32)
        grads[which][:, start : start + whole] = grad
        term = jnp.sum(grad * weights[which][:, start : start + whole].astype(F32), axis=1, keepdims=True)
        total = term if total is None else total + term
    gain_grad[...] = total / gain[...]


def join_columns(shares, weights, gain, size, pad, plan):
    rows = weights[0].shape[0]
    whole = size * len(plan)
    spots = [(i, start) for i, weight in enumerate(weights) for start in range(0, weight.shape[1], whole)]
    count = len(weights)
    gain = gain.astype(F32).reshape(rows, 1)
    if rows % 16:
        total, grads = None, [[] for _ in weights]
        for part, (which, start) in enumerate(spots):
            pieces = [shares[g, :, part * pad + z * size : part * pad + (z + 1) * size] for g, z in plan]
            grads[which].append(jnp.concatenate(pieces, axis=1).astype(F32))
            weight = weights[which][:, start : start + whole].astype(F32)
            term = jnp.sum(grads[which][-1] * weight, axis=1, keepdims=True)
            total = term if total is None else total + term
        return [jnp.concatenate(g, axis=1) for g in grads], (total / gain).reshape(rows)
    out = pl.pallas_call(
        lambda *refs: join_body(plan, spots, size, pad, *refs),
        out_shape=[jax.ShapeDtypeStruct(w.shape, F32) for w in weights] + [jax.ShapeDtypeStruct((rows, 1), F32)],
        compiler_params=pltpu.CompilerParams(vmem_limit_bytes=32 * 2**20),
        cost_estimate=pl.CostEstimate(flops=0, bytes_accessed=8 * 2**20, transcendentals=0),
        name="join_columns",
    )(shares, *weights, gain)
    return out[:count], out[count].reshape(rows)


def mix_forward_body(cpad, slots, span, edge, place, x0, x1, e0, e1, w, gain, taps, a, bcx, o_out):
    def normal(ref):
        x = ref[0].astype(F32)
        return (x * rms_scale(x) * gain[...]).astype(BF)

    rows = slots * span
    a0, a1 = normal(x0), normal(x1)
    a[0, 0] = a0
    a[0, 1] = a1
    edges = dot(jnp.concatenate([normal(e0), normal(e1)], axis=0), w[...])
    bcx[0, 2 * rows :] = edges
    past = edges[:edge, :cpad] * edges[:edge, 2 * cpad :]
    low, high = dot(a0, w[...]), dot(a1, w[...])
    bcx[0, :rows] = low
    bcx[0, rows : 2 * rows] = high
    for slot in range(slots):
        both = [part[slot * span : (slot + 1) * span] for part in (low, high)]
        b, c, v = (
            jnp.concatenate([part[:, i * cpad : (i + 1) * cpad] for part in both], axis=0) for i in range(3)
        )
        bx = b * v
        by_two, by_one = earlier(bx, past[2 * slot : 2 * slot + 1], past[2 * slot + 1 : 2 * slot + 2])
        conv = taps[0:1] * by_two + taps[1:2] * by_one + taps[2:3] * bx
        o = (c * conv).astype(BF)
        o_out[0, 0, slot * span : (slot + 1) * span] = o[:span]
        o_out[0, 1, slot * span : (slot + 1) * span] = o[span:]


def mix_forward(x_all, w_in, gain, taps, place, sides, slots, span, edge):
    width = x_all.shape[2]
    cpad = w_in.shape[1] // 3
    rows = slots * span
    total = 2 * rows + 2 * edge

    def main(y):
        return pl.BlockSpec((1, rows, width), lambda g, r: (r[2 * g + y], 0, 0))

    def rim(y):
        return pl.BlockSpec((1, edge, width), lambda g, r: (r[2 * g + y], rows // edge, 0))

    def fixed(shape):
        return pl.BlockSpec(shape, lambda g, r: (0,) * len(shape))

    return pl.pallas_call(
        lambda *refs: mix_forward_body(cpad, slots, span, edge, *refs),
        grid_spec=pltpu.PrefetchScalarGridSpec(
            num_scalar_prefetch=1,
            grid=(sides,),
            in_specs=[main(0), main(1), rim(0), rim(1), fixed(w_in.shape), fixed(gain.shape), fixed(taps.shape)],
            out_specs=[
                pl.BlockSpec((1, 2, rows, width), lambda g, r: (g, 0, 0, 0)),
                pl.BlockSpec((1, total, 3 * cpad), lambda g, r: (g, 0, 0)),
                pl.BlockSpec((1, 2, rows, cpad), lambda g, r: (g, 0, 0, 0)),
            ],
        ),
        out_shape=[
            jax.ShapeDtypeStruct((sides, 2, rows, width), BF),
            jax.ShapeDtypeStruct((sides, total, 3 * cpad), F32),
            jax.ShapeDtypeStruct((sides, 2, rows, cpad), BF),
        ],
        compiler_params=pltpu.CompilerParams(vmem_limit_bytes=56 * 2**20),
        cost_estimate=pl.CostEstimate(
            flops=sides * total * width * 6 * cpad, bytes_accessed=32 * 2**20, transcendentals=0
        ),
        name="mix_forward",
    )(place, x_all, x_all, x_all, x_all, w_in, gain, taps)


def mix_backward_body(
    cpad, slots, span, edge, nat, d0, d1, e1, a, bcx, w, taps, d_part, da_near, da_far, conv_grad, total, grads
):
    step = pl.program_id(0)
    rows = slots * span
    first = step == 0

    @pl.when(first)
    def _():
        conv_grad[...] = jnp.zeros_like(conv_grad)

    edges = bcx[0, 2 * rows :]
    past = edges[:edge, :cpad] * edges[:edge, 2 * cpad :]
    future = e1[0].astype(F32) * edges[edge:, cpad : 2 * cpad]
    sums = [None, None, None]
    for slot in range(slots):
        spots = [slice(y * rows + slot * span, y * rows + (slot + 1) * span) for y in range(2)]
        b, c, v = (
            jnp.concatenate([bcx[0, s, i * cpad : (i + 1) * cpad] for s in spots], axis=0) for i in range(3)
        )
        here = slice(slot * span, (slot + 1) * span)
        d_o = jnp.concatenate([d0[0, here], d1[0, here]], axis=0).astype(F32)
        bx = b * v
        by_two, by_one = earlier(bx, past[2 * slot : 2 * slot + 1], past[2 * slot + 1 : 2 * slot + 2])
        conv = taps[0:1] * by_two + taps[1:2] * by_one + taps[2:3] * bx
        d_c = d_o * conv
        d_conv = d_o * c
        next_one, next_two = later(d_conv, future[2 * slot : 2 * slot + 1], future[2 * slot + 1 : 2 * slot + 2])
        d_bx = taps[2:3] * d_conv + taps[1:2] * next_one + taps[0:1] * next_two
        for i, part in enumerate((d_bx * v, d_c, d_bx * b)):
            part = part.astype(BF)
            grads[spots[0], i * cpad : (i + 1) * cpad] = part[:span]
            grads[spots[1], i * cpad : (i + 1) * cpad] = part[span:]
        for i, term in enumerate((by_two, by_one, bx)):
            term = jnp.sum(d_conv * term, axis=0, keepdims=True)
            sums[i] = term if sums[i] is None else sums[i] + term
    for i in range(3):
        conv_grad[i : i + 1] += sums[i]
    low = dot_nt(grads[:rows], w[...]).astype(BF)
    high = dot_nt(grads[rows:], w[...]).astype(BF)
    even = nat[0] % 2 == 0
    far = step < pl.num_programs(0) // 2

    def keep(ref):
        @pl.when(even)
        def _():
            ref[0, 0] = low
            ref[0, 1] = high

        @pl.when(jnp.logical_not(even))
        def _():
            ref[0, 0] = high
            ref[0, 1] = low

    @pl.when(far)
    def _():
        keep(da_far)

    @pl.when(jnp.logical_not(far))
    def _():
        keep(da_near)

    term = dot_tn(a[...].reshape(2 * rows, a.shape[-1]), grads[...])

    @pl.when(first)
    def _():
        total[...] = term

    @pl.when(jnp.logical_not(first))
    def _():
        total[...] += term

    @pl.when(step == pl.num_programs(0) - 1)
    def _():
        d_part[...] = total[...].astype(BF)


def mix_backward(do_all, do_rim, a_all, bcx, w_in, taps, nat, sides, slots, span, edge):
    width = w_in.shape[0]
    cpad = w_in.shape[1] // 3
    rows = slots * span
    chips = sides // 2

    def side(i, r):
        return r[2 * ((i + chips) % sides)] // 2

    def main(y):
        return pl.BlockSpec((1, rows, cpad), lambda i, r: (2 * side(i, r) + y, 0, 0))

    def fixed(shape):
        return pl.BlockSpec(shape, lambda i, r: (0,) * len(shape))

    da_shape = jax.ShapeDtypeStruct((chips, 2, rows, width), BF)
    work = sides * 2 * rows * width * 3 * cpad * 4
    return pl.pallas_call(
        lambda *refs: mix_backward_body(cpad, slots, span, edge, *refs),
        grid_spec=pltpu.PrefetchScalarGridSpec(
            num_scalar_prefetch=1,
            grid=(sides,),
            in_specs=[
                main(0),
                main(1),
                pl.BlockSpec((1, edge, cpad), lambda i, r: (side(i, r), 0, 0)),
                pl.BlockSpec((1, 2, rows, width), lambda i, r: (side(i, r), 0, 0, 0)),
                pl.BlockSpec((1, 2 * rows + 2 * edge, 3 * cpad), lambda i, r: (side(i, r), 0, 0)),
                fixed(w_in.shape),
                fixed(taps.shape),
            ],
            out_specs=[
                fixed((width, 3 * cpad)),
                pl.BlockSpec((1, 2, rows, width), lambda i, r: (jnp.maximum(i - chips, 0), 0, 0, 0)),
                pl.BlockSpec((1, 2, rows, width), lambda i, r: (jnp.minimum(i, chips - 1), 0, 0, 0)),
                fixed((8, cpad)),
            ],
            scratch_shapes=[pltpu.VMEM((width, 3 * cpad), F32), pltpu.VMEM((2 * rows, 3 * cpad), BF)],
        ),
        out_shape=[
            jax.ShapeDtypeStruct((width, 3 * cpad), BF),
            da_shape,
            da_shape,
            jax.ShapeDtypeStruct((8, cpad), F32),
        ],
        compiler_params=pltpu.CompilerParams(vmem_limit_bytes=60 * 2**20),
        cost_estimate=pl.CostEstimate(flops=work, bytes_accessed=40 * 2**20, transcendentals=0),
        name="mix_backward",
    )(nat, do_all, do_all, do_rim, a_all, bcx, w_in, taps)


def attend_body(count, o, w, x, gain, o_cat, h1, a2):
    joined = jnp.concatenate([o[t] for t in range(count)], axis=1)
    o_cat[...] = joined
    total = x[...].astype(F32) + dot(joined, w[...])
    h1[...] = total
    a2[...] = (total * rms_scale(total) * gain[...]).astype(BF)


def attend(o, w_out, x, gain, block):
    count, rows, cpad = o.shape
    width = w_out.shape[1]

    def row(last):
        return pl.BlockSpec((block, last), lambda i: (i, 0))

    def fixed(shape):
        return pl.BlockSpec(shape, lambda i: (0,) * len(shape))

    return pl.pallas_call(
        lambda *refs: attend_body(count, *refs),
        grid=(rows // block,),
        in_specs=[
            pl.BlockSpec((count, block, cpad), lambda i: (0, i, 0)),
            fixed(w_out.shape),
            row(width),
            fixed(gain.shape),
        ],
        out_specs=[row(count * cpad), row(width), row(width)],
        out_shape=[
            jax.ShapeDtypeStruct((rows, count * cpad), BF),
            jax.ShapeDtypeStruct((rows, width), F32),
            jax.ShapeDtypeStruct((rows, width), BF),
        ],
        compiler_params=pltpu.CompilerParams(vmem_limit_bytes=40 * 2**20),
        cost_estimate=pl.CostEstimate(
            flops=2 * rows * width * count * cpad, bytes_accessed=14 * 2**20, transcendentals=0
        ),
        name="attend",
    )(o, w_out, x, gain)


def turn_body(count, terms, *refs):
    da2 = refs[0][0].astype(F32)
    for ref in refs[1:terms]:
        da2 = da2 + ref[0].astype(F32)
    d_out, h1, gain, w, dh1, datt, d_o = refs[terms:]
    values = h1[...]
    grad = d_out[...].astype(F32) + norm_back(da2, values, rms_scale(values), gain[...])
    dh1[...] = grad
    low = grad.astype(BF)
    datt[...] = low
    cpad = w.shape[0] // count
    for t in range(count):
        d_o[t] = dot_nt(low, w[t * cpad : (t + 1) * cpad]).astype(BF)


def turn(terms, d_out, h1, gain, w_out, count, block):
    rows, width = h1.shape
    cpad = w_out.shape[0] // count

    def row(last):
        return pl.BlockSpec((block, last), lambda i: (i, 0))

    def fixed(shape):
        return pl.BlockSpec(shape, lambda i: (0,) * len(shape))

    return pl.pallas_call(
        lambda *refs: turn_body(count, len(terms), *refs),
        grid=(rows // block,),
        in_specs=[pl.BlockSpec((1, block, width), lambda i: (0, i, 0))] * len(terms)
        + [row(width), row(width), fixed(gain.shape), fixed(w_out.shape)],
        out_specs=[row(width), row(width), pl.BlockSpec((count, block, cpad), lambda i: (0, i, 0))],
        out_shape=[
            jax.ShapeDtypeStruct((rows, width), F32),
            jax.ShapeDtypeStruct((rows, width), BF),
            jax.ShapeDtypeStruct((count, rows, cpad), BF),
        ],
        compiler_params=pltpu.CompilerParams(vmem_limit_bytes=40 * 2**20),
        cost_estimate=pl.CostEstimate(
            flops=2 * rows * width * count * cpad, bytes_accessed=20 * 2**20, transcendentals=0
        ),
        name="turn",
    )(*terms, d_out, h1, gain, w_out)


def finish_body(terms, *refs):
    da = refs[0][0].astype(F32)
    for ref in refs[1:terms]:
        da = da + ref[0].astype(F32)
    x, dh1, gain, out = refs[terms:]
    values = x[...].astype(F32)
    out[...] = dh1[...] + norm_back(da, values, rms_scale(values), gain[...])


def finish(terms, x, dh1, gain, block):
    rows, width = dh1.shape
    spec = pl.BlockSpec((block, width), lambda i: (i, 0))
    return pl.pallas_call(
        lambda *refs: finish_body(len(terms), *refs),
        grid=(rows // block,),
        in_specs=[pl.BlockSpec((1, block, width), lambda i: (0, i, 0))] * len(terms)
        + [spec] * 2
        + [pl.BlockSpec(gain.shape, lambda i: (0, 0))],
        out_specs=spec,
        out_shape=jax.ShapeDtypeStruct((rows, width), F32),
        compiler_params=pltpu.CompilerParams(vmem_limit_bytes=40 * 2**20),
        cost_estimate=pl.CostEstimate(flops=rows * width * 8, bytes_accessed=12 * 2**20, transcendentals=0),
        name="finish",
    )(*terms, x, dh1, gain)


def feed_body(hid, hpad, a2, d_out, w_both, w_down, *refs):
    m, d_both, f, da2 = refs[-4:]
    gu = dot(a2[0], w_both[...])
    gate, up = gu[:, :hid], gu[:, hpad : hpad + hid]
    dm = dot_nt(d_out[0], w_down[...])
    sigma = 1.0 / (1.0 + jnp.exp(-gate))
    active = gate * sigma
    inner = (active * up).astype(BF)
    m[0] = inner
    if hpad > hid:
        none = jnp.zeros((gu.shape[0], hpad - hid), BF)
        d_both[0, :, hid:hpad] = none
        d_both[0, :, hpad + hid :] = none
    d_both[0, :, :hid] = (dm * up * (sigma * (1.0 + gate * (1.0 - sigma)))).astype(BF)
    d_both[0, :, hpad : hpad + hid] = (dm * active).astype(BF)
    f[0] = dot(inner, w_down[...]).astype(BF)
    da2[0] = dot_nt(d_both[0], w_both[...]).astype(BF)


def feed(a2_all, d_all, w_both, w_down, first, kept=()):
    blocks, rows, width = a2_all.shape
    half = blocks // 2
    hid, hpad = w_down.shape[0], w_both.shape[1] // 2

    def part(last):
        return pl.BlockSpec((1, rows, last), lambda i: (i + first, 0, 0))

    def fixed(shape):
        return pl.BlockSpec(shape, lambda i: (0,) * len(shape), pipeline_mode=pl.Buffered(1))

    own = pl.BlockSpec((1, rows, width), lambda i: (i, 0, 0))
    return pl.pallas_call(
        lambda *refs: feed_body(hid, hpad, *refs),
        grid=(half,),
        in_specs=[part(width), part(width), fixed(w_both.shape), fixed(w_down.shape)]
        + [pl.BlockSpec(memory_space=pl.ANY)] * len(kept),
        out_specs=[part(hid), part(2 * hpad), own, own],
        out_shape=[
            jax.ShapeDtypeStruct((blocks, rows, hid), BF),
            jax.ShapeDtypeStruct((blocks, rows, 2 * hpad), BF),
            jax.ShapeDtypeStruct((half, rows, width), BF),
            jax.ShapeDtypeStruct((half, rows, width), BF),
        ],
        input_output_aliases={4 + i: i for i in range(len(kept))},
        compiler_params=pltpu.CompilerParams(vmem_limit_bytes=60 * 2**20),
        cost_estimate=pl.CostEstimate(
            flops=half * rows * width * hid * 12, bytes_accessed=40 * 2**20, transcendentals=half * rows * hid
        ),
        name="feed",
    )(a2_all, d_all, w_both, w_down, *kept)


def on_device(
    tokens,
    cotangent,
    lengths,
    in_weight,
    conv_weight,
    out_weight,
    gain_one,
    gain_two,
    gate_weight,
    up_weight,
    down_weight,
):
    nx, nc, nz, ny = (lax.axis_size(name) for name in ("x", "c", "z", "y"))
    sizes = (nx, nc, ny)
    ndp = nx * nc
    slots, span, width = tokens.shape
    conv_weight_early = conv_weight
    rows = slots * span
    own_in = in_weight.shape[0]
    own_hid = down_weight.shape[0]
    chan, hid = nz * own_in, nz * own_hid
    cpad, hpad = up_to(chan + 2, 128), up_to(hid, 128)
    edge = up_to(2 * slots, 16)
    hops = [(dx, dc, dy) for dc in range(nc) for dx in range(nx) for dy in range(ny)]
    sides = ndp
    line = Line(nz)
    row_y = lax.axis_index("y")
    here = [lax.axis_index(name) for name in GROUP]
    place = []
    for i in range(nx):
        for j in range(nc):
            for k in range(ny):
                far = [(to + n - at) % n for to, at, n in zip((i, j, k), here, sizes)]
                place.append((far[1] * nx + far[0]) * ny + far[2])
    place = jnp.stack(place).astype(jnp.int32)
    turn_at = []
    for dx, dc, dy in hops:
        at = [(at + far) % n for at, far, n in zip(here, (dx, dc, dy), sizes)]
        turn_at.append((at[0] * nc + at[1]) * ny + at[2])
    nat = jnp.stack(turn_at).astype(jnp.int32)
    first = (lax.axis_index("z") * ny + row_y) * span
    positions = first + jnp.arange(span, dtype=jnp.int32)
    mask = (positions[None, :] < lengths[:, None]).astype(F32).reshape(rows, 1)
    rim_route = []
    for z in range(nz - 1):
        rim_route += [(z * ny + 1, (z + 1) * ny), ((z + 1) * ny, z * ny + 1)]
    down_route = [(z + 1, z) for z in range(nz - 1)]

    def stack_sides(parts):
        near = stack([parts[h] for h in hops[:sides]], len(hops))
        return stack([parts[h] for h in hops[sides:]], len(hops), sides, near)

    def rim(values, start):
        count, last = values.shape[0], values.shape[-1]
        some = values.reshape(count, slots, span, last)[:, :, start : start + 2].reshape(count, 2 * slots, last)
        return jnp.pad(some, ((0, 0), (0, edge - 2 * slots), (0, 0)))

    x_bf = tokens.reshape(rows, width)
    x = x_bf.astype(F32)
    d_out_bf = (mask * cotangent.reshape(rows, width).astype(F32)).astype(BF)

    hold = lax.optimization_barrier
    plan = shuffle_plan(ndp, nz, ny)

    gains = jnp.stack([gain_one, gain_two], axis=1)
    cut = cut_columns([in_weight], own_in, cpad, plan, gains)
    cut = lax.all_to_all(cut, GROUP, 0, 0, tiled=True).reshape(ndp, ny, own_in, 3 * cpad)
    taps_here = jnp.pad(conv_weight.T, ((0, 0), (0, 128 - conv_weight.shape[0])))
    w_out = line.fetch_all(jnp.concatenate([out_weight, taps_here], axis=1))
    pairs = tokens.reshape(slots, span, width)
    pairs = jnp.where(row_y == 0, pairs[:, :2], pairs[:, -2:]).reshape(2 * slots, width)
    x_rim = lax.ppermute(jnp.pad(pairs, ((0, edge - 2 * slots), (0, 0))), ("z", "y"), rim_route)
    (cut, x_rim), (x_late, gate_late) = after((cut, x_rim), (x_bf, gate_weight))
    x_late = jnp.concatenate([x_late, x_rim], axis=0)

    w_in = lax.all_gather(cut.reshape(ndp, ny * own_in, 3 * cpad), "z", axis=1, tiled=True).reshape(width, 3 * cpad)
    w_out = line.place(w_out, 0).reshape(chan, width + 128)
    taps = w_out[:, width : width + 8].astype(F32).T
    taps = jnp.pad(taps, ((0, 0), (0, cpad - chan)))
    w_out = w_out[:, :width]
    x_all = near_gather(x_late, sizes)
    both = cut_columns([gate_late, up_weight], own_hid, hpad, plan)
    both = lax.all_to_all(both, GROUP, 0, 0, tiled=True).reshape(ndp, ny * own_in, 2 * hpad)
    x_all, both, w_out = hold((x_all, both, w_out))

    w_both = lax.all_gather(both, "z", axis=1, tiled=True).reshape(width, 2 * hpad)
    x_all = far_gather(x_all, sizes)
    gain_a = w_in[:, chan].astype(F32).reshape(1, width)
    gain_b = w_in[:, chan + 1].astype(F32).reshape(1, width)
    x_all, (w_out, d_late) = after(x_all, (w_out, d_out_bf))

    w_out = near_gather(w_out, sizes)
    x_all = stack_sides(x_all)
    d_all = near_gather(d_late, sizes)
    a_all, bcx, o_all = mix_forward(x_all, w_in, gain_a, taps, place, sides, slots, span, edge)
    o_all, w_out = hold((o_all, w_out))
    w_out = diag_gather(w_out, sizes)

    o_own = lax.all_to_all(o_all.reshape(len(hops), rows, cpad), GROUP, 0, 0, tiled=True)
    w_some = cross_gather(w_out, sizes)
    w_out = jnp.zeros((len(hops), cpad, width), BF)
    for i, h in enumerate(hops):
        w_out = lax.dynamic_update_slice(w_out, w_some[h][None], (turn_at[i], 0, 0))
    w_out = w_out.reshape(len(hops) * cpad, width)
    o_own, w_out = hold((o_own, w_out))

    block = rows // 2
    o_cat, h1, a2 = attend(o_own, w_out, x_bf, gain_b, block)
    (_, w_both), down_weight = after((a2, w_both), down_weight)

    w_down = lax.all_gather(down_weight, "z", axis=0, tiled=True)
    a2_all = near_gather(a2, sizes)
    d_all = cross_gather(diag_gather(d_all, sizes), sizes)
    a2_all, d_all = hold((a2_all, d_all))
    d_all = stack([d_all[h] for h in hops])
    a2_all, d_all = hold((diag_gather(a2_all, sizes), d_all))
    a2_all = cross_gather(a2_all, sizes)
    a2_all = stack_sides(a2_all)

    m, d_both, f_far, da_far = feed(a2_all, d_all, w_both, w_down, len(hops) // 2)
    m, d_both, f_near, da_near = feed(a2_all, d_all, w_both, w_down, 0, (m, d_both))
    da2 = GroupSum(da_near, da_far, sizes)
    f = GroupSum(f_near, f_far, sizes)
    d_flat = d_all.reshape(-1, width)
    da2.sum_far()
    da2.total, m = after(da2.total, m)
    da2.send_far()
    down_part = dot_tn(m.reshape(-1, hid), d_flat).astype(BF)
    da2.more, f.cross, down_part = hold((da2.more, f.cross, down_part))

    da2.sum_near()
    da2.total, d_both = after(da2.total, d_both)
    da2.send_near()
    both_part = dot_tn(a2_all.reshape(-1, width), d_both.reshape(-1, 2 * hpad)).astype(BF)
    da2.last, both_part, f.cross = hold((da2.last, both_part, f.cross))
    both_sum = lax.psum_scatter(
        both_part.reshape(ndp, nz * ny * own_in, 2 * hpad), "z", scatter_dimension=1, tiled=True
    )

    f.sum_far()
    da2.last, f.total = hold((da2.last, f.total))
    f.send_far()
    dh1, datt, do_own = turn(da2.terms(), d_out_bf, h1, gain_b, w_out, len(hops), block)
    do_own, datt, f.more = hold((do_own, datt, f.more))

    do_all = lax.all_to_all(do_own, GROUP, 0, 0, tiled=True)
    out_part = dot_tn(o_cat, datt).astype(BF).reshape(len(hops), cpad, width)[:, :chan]
    out_near = jnp.stack([lax.dynamic_index_in_dim(out_part, t, 0, keepdims=False) for t in turn_at[:ndp]], axis=0)
    out_far = jnp.stack([lax.dynamic_index_in_dim(out_part, t, 0, keepdims=False) for t in turn_at[ndp:]], axis=0)
    out = GroupSum(out_near, out_far, sizes)
    f.sum_near()
    do_all, out.cross, f.total = hold((do_all, out.cross, f.total))

    do_rim = lax.ppermute(rim(do_all.reshape(sides, ny, rows, cpad)[:, 0], 0), "z", down_route)
    out.sum_far()
    do_rim, f.total, out.total = hold((do_rim, f.total, out.total))

    f.send_near()
    out.send_far()
    in_part, da_near, da_far, conv_part = mix_backward(
        do_all, do_rim, a_all, bcx, w_in, taps, nat, sides, slots, span, edge
    )
    (in_part, da_near, da_far, conv_part), f.last, out.more = hold(
        ((in_part, da_near, da_far, conv_part), f.last, out.more)
    )

    flat = (ndp, rows, width)
    da = GroupSum(da_near.reshape(flat), da_far.reshape(flat), sizes)
    in_part, both_sum = hold((in_part, both_sum))
    in_sum = lax.psum_scatter(
        in_part.reshape(ndp, nz * ny * own_in, 3 * cpad), "z", scatter_dimension=1, tiled=True
    )
    both_sum = lax.all_to_all(both_sum.reshape(ndp * ny, own_in, 2 * hpad), GROUP, 0, 0, tiled=True)
    da.cross = hold(da.cross)

    da.sum_far()
    da.send_far()
    out.sum_near()
    out.send_near()
    da.more = hold(da.more)
    da.sum_near()
    _, in_sum, both_sum, out.last = hold((da.total, in_sum, both_sum, out.last))
    in_sum, down_part = after(in_sum, down_part)
    down_grad = lax.psum_scatter(down_part, "z", scatter_dimension=0, tiled=True)
    da.send_near()
    in_sum = lax.all_to_all(in_sum.reshape(ndp * ny, own_in, 3 * cpad), GROUP, 0, 0, tiled=True)
    out_sum = sum(term[0].astype(F32) for term in out.terms()).astype(BF)
    out_grad = line.reduce_direct(out_sum.reshape(nz, own_in, width), 0)
    conv_grad = line.reduce_direct(conv_part[:3, :chan].reshape(3, nz, own_in), 1)
    total = h1
    for term in f.terms():
        total = total + term[0].astype(F32)
    mixed = (mask * total).astype(BF)
    (gate_grad, up_grad), gain_two_grad = join_columns(
        both_sum, [gate_weight, up_weight], gain_two, own_hid, hpad, plan
    )
    in_sum, da.last, mixed, gate_grad, up_grad = hold((in_sum, da.last, mixed, gate_grad, up_grad))

    input_grad = finish(da.terms(), x_bf, dh1, gain_a, block)
    out_grad = sum(term.astype(F32) for term in out_grad)
    conv_grad = sum(conv_grad)
    (in_grad,), gain_one_grad = join_columns(in_sum, [in_weight], gain_one, own_in, cpad, plan)
    down_grad = down_grad.astype(F32)
    return (
        mixed.reshape(slots, span, width),
        input_grad.reshape(slots, span, width),
        in_grad,
        conv_grad,
        out_grad,
        gain_one_grad,
        gain_two_grad,
        gate_grad,
        up_grad,
        down_grad,
    )


def solution(mesh):
    dp, seq = mesh.shape["dp"], mesh.shape["seq"]
    fine = Mesh(mesh.devices.reshape(dp // 2, 2, seq // 2, 2), ("x", "c", "z", "y"))
    slot, place = ("x", "c"), ("z", "y")
    every = slot + place
    in_specs = (
        P(slot, place, None),
        P(slot, place, None),
        P(slot),
        P(every, None),
        P(None, every),
        P(every, None),
        P(every),
        P(every),
        P(every, None),
        P(every, None),
        P(every, None),
    )
    out_specs = (
        P(slot, place, None),
        P(slot, place, None),
        P(every, None),
        P(None, every),
        P(every, None),
        P(every),
        P(every),
        P(every, None),
        P(every, None),
        P(every, None),
    )
    return jax.shard_map(
        on_device, mesh=fine, in_specs=in_specs, out_specs=out_specs, check_vma=False
    )
```

```python
import jax
import jax.numpy as jnp
from jax import lax
from jax.experimental import pallas as pl
from jax.experimental.pallas import tpu as pltpu
from jax.sharding import Mesh
from jax.sharding import PartitionSpec as P

BF = jnp.bfloat16
F32 = jnp.float32
GROUP = ("x", "c", "y")


def ring_of(count):
    return [0] + list(range(1, count, 2)) + list(range(count - 2 + count % 2, 0, -2))


def send(block, hop, sizes):
    nx, nc, ny = sizes
    dx, dc, dy = hop
    route = []
    for i in range(nx):
        for j in range(nc):
            for k in range(ny):
                source = (i * nc + j) * ny + k
                target = (((i + dx) % nx) * nc + (j + dc) % nc) * ny + (k + dy) % ny
                route.append((source, target))
    return lax.ppermute(block, GROUP, route)


def mirror(hop, sizes):
    return tuple((-h) % n for h, n in zip(hop, sizes))


def fetch(block, hop, sizes):
    return send(block, mirror(hop, sizes), sizes)


def near_gather(block, sizes):
    nx, nc, ny = sizes
    got = {(0, 0): block}
    for dx in range(1, nx):
        got[dx, 0] = fetch(block, (dx, 0, 0), sizes)
    for dy in range(1, ny):
        got[0, dy] = fetch(block, (0, 0, dy), sizes)
    return got


def diag_gather(got, sizes):
    nx, _, ny = sizes
    half = got[0, 0].shape[0] // 2
    got = dict(got)
    for dx in range(1, nx):
        for dy in range(1, ny):
            one = fetch(got[dx, 0][:half], (0, 0, dy), sizes)
            two = fetch(got[0, dy][half:], (dx, 0, 0), sizes)
            got[dx, dy] = jnp.concatenate([one, two], axis=0)
    return got


def cross_gather(got, sizes):
    full = {}
    for (dx, dy), value in got.items():
        full[dx, 0, dy] = value
        for dc in range(1, sizes[1]):
            full[dx, dc, dy] = fetch(value, (0, dc, 0), sizes)
    return full


def far_gather(got, sizes):
    return cross_gather(diag_gather(got, sizes), sizes)


def stack(blocks, count=None, first=0, kept=None):
    here = len(blocks)
    count = count or here
    more = [] if kept is None else [kept]

    def body(*refs):
        parts, (out, held, came, left) = refs[:here], refs[-4:]
        ins = [pltpu.make_async_copy(parts[i], held.at[i], came.at[i]) for i in range(here)]
        outs = [pltpu.make_async_copy(held.at[i], out.at[first + i], left.at[i]) for i in range(here)]
        for copy in ins:
            copy.start()
        for i in range(here):
            ins[i].wait()
            outs[i].start()
        for copy in outs:
            copy.wait()

    return pl.pallas_call(
        body,
        in_specs=[pl.BlockSpec(memory_space=pl.ANY)] * (here + len(more)),
        out_specs=pl.BlockSpec(memory_space=pl.ANY),
        out_shape=jax.ShapeDtypeStruct((count, *blocks[0].shape), blocks[0].dtype),
        input_output_aliases={here: 0} if more else {},
        scratch_shapes=[
            pltpu.VMEM((here, *blocks[0].shape), blocks[0].dtype),
            pltpu.SemaphoreType.DMA((here,)),
            pltpu.SemaphoreType.DMA((here,)),
        ],
        compiler_params=pltpu.CompilerParams(vmem_limit_bytes=60 * 2**20),
        cost_estimate=pl.CostEstimate(flops=0, bytes_accessed=4 * here * blocks[0].size, transcendentals=0),
        name="stack",
    )(*blocks, *more)


def merge(near, cross, at, one=None, two=None):
    _, rows, width = near.shape
    half = rows // 2
    extra = [] if one is None else [one, two]

    def body(*refs):
        total = refs[0][0].astype(F32) + refs[1][0].astype(F32)
        if extra:
            upper = pl.program_id(0) == 0
            total = total + jnp.where(upper, refs[2][...], refs[3][...]).astype(F32)
        refs[-1][...] = total.astype(BF)

    block = pl.BlockSpec((1, half, width), lambda i: (at, i, 0))
    return pl.pallas_call(
        body,
        grid=(2,),
        in_specs=[block, block] + [pl.BlockSpec((half, width), lambda i: (0, 0))] * len(extra),
        out_specs=pl.BlockSpec((half, width), lambda i: (i, 0)),
        out_shape=jax.ShapeDtypeStruct((rows, width), BF),
        compiler_params=pltpu.CompilerParams(vmem_limit_bytes=24 * 2**20),
        cost_estimate=pl.CostEstimate(flops=3 * rows * width, bytes_accessed=10 * rows * width, transcendentals=0),
        name="merge",
    )(near, cross, *extra)


class GroupSum:
    def __init__(self, near, far, sizes):
        nx, _, ny = sizes
        self.sizes = sizes
        self.keys = [(dx, dy) for dx in range(nx) for dy in range(ny)]
        self.near = near
        self.cross = send(far, (0, 1, 0), sizes)
        self.more, self.last = {}, {}

    def sum_far(self):
        self.total = {
            key: merge(self.near, self.cross, i) for i, key in enumerate(self.keys) if key[0] and key[1]
        }

    def send_far(self):
        for (dx, dy), total in self.total.items():
            half = total.shape[0] // 2
            self.more[dx, dy] = (
                send(total[:half], (dx, 0, 0), self.sizes),
                send(total[half:], (0, 0, dy), self.sizes),
            )

    def sum_near(self):
        self.total = {}
        for i, key in enumerate(self.keys):
            if (key[0] == 0) == (key[1] == 0):
                continue
            low = [one for (dx, dy), (one, _) in self.more.items() if key == (0, dy)]
            high = [two for (dx, dy), (_, two) in self.more.items() if key == (dx, 0)]
            none = jnp.zeros((self.near.shape[1] // 2, self.near.shape[2]), BF)
            low = sum(v.astype(F32) for v in low[1:]) + low[0].astype(F32) if len(low) > 1 else (low + [none])[0]
            high = sum(v.astype(F32) for v in high[1:]) + high[0].astype(F32) if len(high) > 1 else (high + [none])[0]
            self.total[key] = merge(self.near, self.cross, i, low.astype(BF), high.astype(BF))

    def send_near(self):
        for key, total in self.total.items():
            self.last[key] = send(total, (key[0], 0, key[1]), self.sizes)

    def terms(self):
        return [self.near, self.cross] + [v[None] for v in self.last.values()]


class Line:
    def __init__(self, count):
        self.count = count
        self.ring = ring_of(count)
        self.route = [(self.ring[i], self.ring[(i + 1) % count]) for i in range(count)]
        place = {z: i for i, z in enumerate(self.ring)}
        table = [[self.ring[(place[z] - s) % count] for z in range(count)] for s in range(count + 1)]
        here = lax.axis_index("z")
        self.source = [here]
        for s in range(1, count + 1):
            at = jnp.int32(table[s][0])
            for z in range(1, count):
                at = jnp.where(here == z, jnp.int32(table[s][z]), at)
            self.source.append(at)

    def gather(self, block, axis):
        shape = list(block.shape)
        shape.insert(axis, self.count)
        full = jnp.zeros(shape, block.dtype)
        for s in range(self.count):
            if s > 0:
                block = lax.ppermute(block, "z", self.route)
            full = lax.dynamic_update_slice_in_dim(full, jnp.expand_dims(block, axis), self.source[s], axis)
        return full

    def fetch_all(self, block):
        got = [block]
        for s in range(1, self.count):
            route = [(self.ring[i], self.ring[(i + s) % self.count]) for i in range(self.count)]
            got.append(lax.ppermute(block, "z", route))
        return got

    def place(self, blocks, axis):
        shape = list(blocks[0].shape)
        shape.insert(axis, self.count)
        full = jnp.zeros(shape, blocks[0].dtype)
        for s, block in enumerate(blocks):
            full = lax.dynamic_update_slice_in_dim(full, jnp.expand_dims(block, axis), self.source[s], axis)
        return full

    def reduce_direct(self, parts, axis, steps=None):
        terms = [lax.dynamic_index_in_dim(parts, self.source[0], axis, keepdims=False)]
        for s in range(1, self.count) if steps is None else steps:
            part = lax.dynamic_index_in_dim(parts, self.source[s], axis, keepdims=False)
            route = [(self.ring[i], self.ring[(i - s) % self.count]) for i in range(self.count)]
            terms.append(lax.ppermute(part, "z", route))
        return terms


def dot(left, right):
    return jnp.dot(left, right, preferred_element_type=F32)


def dot_nt(left, right):
    return lax.dot_general(left, right, (((1,), (1,)), ((), ())), preferred_element_type=F32)


def dot_tn(left, right):
    return lax.dot_general(left, right, (((0,), (0,)), ((), ())), preferred_element_type=F32)


def rms_scale(values):
    return lax.rsqrt(jnp.mean(values * values, axis=-1, keepdims=True) + 1e-05)


def norm_back(gradient, values, scale, gain):
    scaled = gradient * gain
    mean_term = jnp.mean(scaled * values, axis=-1, keepdims=True)
    return scale * scaled - values * scale * scale * scale * mean_term


def after(first, second):
    return lax.optimization_barrier((first, second))


def up_to(count, step):
    return (count + step - 1) // step * step


def earlier(values, one, two):
    rows = lax.broadcasted_iota(jnp.int32, values.shape, 0)
    by_one = jnp.where(rows == 0, two, pltpu.roll(values, 1, 0))
    by_two = jnp.where(rows == 0, one, jnp.where(rows == 1, two, pltpu.roll(values, 2, 0)))
    return by_two, by_one


def later(values, one, two):
    count = values.shape[0]
    rows = lax.broadcasted_iota(jnp.int32, values.shape, 0)
    by_one = jnp.where(rows == count - 1, one, pltpu.roll(values, count - 1, 0))
    by_two = jnp.where(
        rows == count - 1, two, jnp.where(rows == count - 2, one, pltpu.roll(values, count - 2, 0))
    )
    return by_one, by_two


def shuffle_plan(ndp, nz, ny):
    return [(dp * ny + y, z) for dp in range(ndp) for z in range(nz) for y in range(ny)]


def cut_body(plan, spots, size, pad, extra, *refs):
    count = 1 + max(which for which, _ in spots)
    sources, more, out = refs[:count], refs[count:-1], refs[-1]
    share = {}
    for at, (group, z) in enumerate(plan):
        share[group, z] = at
    groups = 1 + max(group for group, _ in plan)
    depth = len(plan) // groups
    for group in range(groups):
        for part, (which, start) in enumerate(spots):
            pieces = [
                sources[which][:, start + share[group, z] * size : start + (share[group, z] + 1) * size]
                for z in range(depth)
            ]
            left = pad - depth * size
            if more and part == 0:
                pieces.append(more[0][...])
                left -= extra
            if left:
                pieces.append(jnp.zeros((pieces[0].shape[0], left), pieces[0].dtype))
            out[group, :, part * pad : (part + 1) * pad] = jnp.concatenate(pieces, axis=1)


def cut_columns(sources, size, pad, plan, more=None):
    rows = sources[0].shape[0]
    whole = size * len(plan)
    spots = [(i, start) for i, source in enumerate(sources) for start in range(0, source.shape[1], whole)]
    parts = len(spots)
    groups = 1 + max(group for group, _ in plan)
    extra = 0 if more is None else more.shape[1]
    if rows % 16:
        order = [[i for z in range(len(plan)) for i, p in enumerate(plan) if p == (g, z)] for g in range(groups)]
        out = []
        for group in order:
            row = []
            for part, (which, start) in enumerate(spots):
                pieces = [sources[which][:, start + i * size : start + (i + 1) * size] for i in group]
                left = pad - len(group) * size
                if more is not None and part == 0:
                    pieces.append(more)
                    left -= extra
                pieces.append(jnp.zeros((rows, left), BF))
                row += pieces
            out.append(jnp.concatenate(row, axis=1))
        return jnp.stack(out, axis=0)
    inputs = list(sources) + ([] if more is None else [more])
    return pl.pallas_call(
        lambda *refs: cut_body(plan, spots, size, pad, extra, *refs),
        out_shape=jax.ShapeDtypeStruct((groups, rows, parts * pad), BF),
        compiler_params=pltpu.CompilerParams(vmem_limit_bytes=32 * 2**20),
        cost_estimate=pl.CostEstimate(flops=0, bytes_accessed=6 * 2**20, transcendentals=0),
        name="cut_columns",
    )(*inputs)


def join_body(plan, spots, size, pad, *refs):
    count = 1 + max(which for which, _ in spots)
    shares, weights, gain = refs[0], refs[1 : 1 + count], refs[1 + count]
    grads, gain_grad = refs[2 + count : 2 + 2 * count], refs[-1]
    whole = size * len(plan)
    total = None
    for part, (which, start) in enumerate(spots):
        pieces = [
            shares[group, :, part * pad + z * size : part * pad + (z + 1) * size] for group, z in plan
        ]
        grad = jnp.concatenate(pieces, axis=1).astype(F32)
        grads[which][:, start : start + whole] = grad
        term = jnp.sum(grad * weights[which][:, start : start + whole].astype(F32), axis=1, keepdims=True)
        total = term if total is None else total + term
    gain_grad[...] = total / gain[...]


def join_columns(shares, weights, gain, size, pad, plan):
    rows = weights[0].shape[0]
    whole = size * len(plan)
    spots = [(i, start) for i, weight in enumerate(weights) for start in range(0, weight.shape[1], whole)]
    count = len(weights)
    gain = gain.astype(F32).reshape(rows, 1)
    if rows % 16:
        total, grads = None, [[] for _ in weights]
        for part, (which, start) in enumerate(spots):
            pieces = [shares[g, :, part * pad + z * size : part * pad + (z + 1) * size] for g, z in plan]
            grads[which].append(jnp.concatenate(pieces, axis=1).astype(F32))
            weight = weights[which][:, start : start + whole].astype(F32)
            term = jnp.sum(grads[which][-1] * weight, axis=1, keepdims=True)
            total = term if total is None else total + term
        return [jnp.concatenate(g, axis=1) for g in grads], (total / gain).reshape(rows)
    out = pl.pallas_call(
        lambda *refs: join_body(plan, spots, size, pad, *refs),
        out_shape=[jax.ShapeDtypeStruct(w.shape, F32) for w in weights] + [jax.ShapeDtypeStruct((rows, 1), F32)],
        compiler_params=pltpu.CompilerParams(vmem_limit_bytes=32 * 2**20),
        cost_estimate=pl.CostEstimate(flops=0, bytes_accessed=8 * 2**20, transcendentals=0),
        name="join_columns",
    )(shares, *weights, gain)
    return out[:count], out[count].reshape(rows)


def mix_forward_body(cpad, slots, span, edge, place, x0, x1, e0, e1, w, gain, taps, a, bcx, o_out):
    def normal(ref):
        x = ref[0].astype(F32)
        return (x * rms_scale(x) * gain[...]).astype(BF)

    rows = slots * span
    a0, a1 = normal(x0), normal(x1)
    a[0, 0] = a0
    a[0, 1] = a1
    edges = dot(jnp.concatenate([normal(e0), normal(e1)], axis=0), w[...])
    bcx[0, 2 * rows :] = edges
    past = edges[:edge, :cpad] * edges[:edge, 2 * cpad :]
    low, high = dot(a0, w[...]), dot(a1, w[...])
    bcx[0, :rows] = low
    bcx[0, rows : 2 * rows] = high
    for slot in range(slots):
        both = [part[slot * span : (slot + 1) * span] for part in (low, high)]
        b, c, v = (
            jnp.concatenate([part[:, i * cpad : (i + 1) * cpad] for part in both], axis=0) for i in range(3)
        )
        bx = b * v
        by_two, by_one = earlier(bx, past[2 * slot : 2 * slot + 1], past[2 * slot + 1 : 2 * slot + 2])
        conv = taps[0:1] * by_two + taps[1:2] * by_one + taps[2:3] * bx
        o = (c * conv).astype(BF)
        o_out[0, 0, slot * span : (slot + 1) * span] = o[:span]
        o_out[0, 1, slot * span : (slot + 1) * span] = o[span:]


def mix_forward(x_all, w_in, gain, taps, place, sides, slots, span, edge):
    width = x_all.shape[2]
    cpad = w_in.shape[1] // 3
    rows = slots * span
    total = 2 * rows + 2 * edge

    def main(y):
        return pl.BlockSpec((1, rows, width), lambda g, r: (r[2 * g + y], 0, 0))

    def rim(y):
        return pl.BlockSpec((1, edge, width), lambda g, r: (r[2 * g + y], rows // edge, 0))

    def fixed(shape):
        return pl.BlockSpec(shape, lambda g, r: (0,) * len(shape))

    return pl.pallas_call(
        lambda *refs: mix_forward_body(cpad, slots, span, edge, *refs),
        grid_spec=pltpu.PrefetchScalarGridSpec(
            num_scalar_prefetch=1,
            grid=(sides,),
            in_specs=[main(0), main(1), rim(0), rim(1), fixed(w_in.shape), fixed(gain.shape), fixed(taps.shape)],
            out_specs=[
                pl.BlockSpec((1, 2, rows, width), lambda g, r: (g, 0, 0, 0)),
                pl.BlockSpec((1, total, 3 * cpad), lambda g, r: (g, 0, 0)),
                pl.BlockSpec((1, 2, rows, cpad), lambda g, r: (g, 0, 0, 0)),
            ],
        ),
        out_shape=[
            jax.ShapeDtypeStruct((sides, 2, rows, width), BF),
            jax.ShapeDtypeStruct((sides, total, 3 * cpad), F32),
            jax.ShapeDtypeStruct((sides, 2, rows, cpad), BF),
        ],
        compiler_params=pltpu.CompilerParams(vmem_limit_bytes=56 * 2**20),
        cost_estimate=pl.CostEstimate(
            flops=sides * total * width * 6 * cpad, bytes_accessed=32 * 2**20, transcendentals=0
        ),
        name="mix_forward",
    )(place, x_all, x_all, x_all, x_all, w_in, gain, taps)


def mix_backward_body(
    cpad, slots, span, edge, nat, d0, d1, e1, a, bcx, w, taps, d_part, da_near, da_far, conv_grad, total, grads
):
    step = pl.program_id(0)
    rows = slots * span
    first = step == 0

    @pl.when(first)
    def _():
        conv_grad[...] = jnp.zeros_like(conv_grad)

    edges = bcx[0, 2 * rows :]
    past = edges[:edge, :cpad] * edges[:edge, 2 * cpad :]
    future = e1[0].astype(F32) * edges[edge:, cpad : 2 * cpad]
    sums = [None, None, None]
    for slot in range(slots):
        spots = [slice(y * rows + slot * span, y * rows + (slot + 1) * span) for y in range(2)]
        b, c, v = (
            jnp.concatenate([bcx[0, s, i * cpad : (i + 1) * cpad] for s in spots], axis=0) for i in range(3)
        )
        here = slice(slot * span, (slot + 1) * span)
        d_o = jnp.concatenate([d0[0, here], d1[0, here]], axis=0).astype(F32)
        bx = b * v
        by_two, by_one = earlier(bx, past[2 * slot : 2 * slot + 1], past[2 * slot + 1 : 2 * slot + 2])
        conv = taps[0:1] * by_two + taps[1:2] * by_one + taps[2:3] * bx
        d_c = d_o * conv
        d_conv = d_o * c
        next_one, next_two = later(d_conv, future[2 * slot : 2 * slot + 1], future[2 * slot + 1 : 2 * slot + 2])
        d_bx = taps[2:3] * d_conv + taps[1:2] * next_one + taps[0:1] * next_two
        for i, part in enumerate((d_bx * v, d_c, d_bx * b)):
            part = part.astype(BF)
            grads[spots[0], i * cpad : (i + 1) * cpad] = part[:span]
            grads[spots[1], i * cpad : (i + 1) * cpad] = part[span:]
        for i, term in enumerate((by_two, by_one, bx)):
            term = jnp.sum(d_conv * term, axis=0, keepdims=True)
            sums[i] = term if sums[i] is None else sums[i] + term
    for i in range(3):
        conv_grad[i : i + 1] += sums[i]
    low = dot_nt(grads[:rows], w[...]).astype(BF)
    high = dot_nt(grads[rows:], w[...]).astype(BF)
    even = nat[0] % 2 == 0
    far = step < pl.num_programs(0) // 2

    def keep(ref):
        @pl.when(even)
        def _():
            ref[0, 0] = low
            ref[0, 1] = high

        @pl.when(jnp.logical_not(even))
        def _():
            ref[0, 0] = high
            ref[0, 1] = low

    @pl.when(far)
    def _():
        keep(da_far)

    @pl.when(jnp.logical_not(far))
    def _():
        keep(da_near)

    term = dot_tn(a[...].reshape(2 * rows, a.shape[-1]), grads[...])

    @pl.when(first)
    def _():
        total[...] = term

    @pl.when(jnp.logical_not(first))
    def _():
        total[...] += term

    @pl.when(step == pl.num_programs(0) - 1)
    def _():
        chan = d_part.shape[1] // 3
        d_part[...] = jnp.concatenate(
            [total[:, i * cpad : i * cpad + chan].astype(BF) for i in range(3)], axis=1
        )


def mix_backward(do_all, do_rim, a_all, bcx, w_in, taps, nat, sides, slots, span, edge, chan):
    width = w_in.shape[0]
    cpad = w_in.shape[1] // 3
    rows = slots * span
    chips = sides // 2

    def side(i, r):
        return r[2 * ((i + chips) % sides)] // 2

    def main(y):
        return pl.BlockSpec((1, rows, cpad), lambda i, r: (2 * side(i, r) + y, 0, 0))

    def fixed(shape):
        return pl.BlockSpec(shape, lambda i, r: (0,) * len(shape))

    da_shape = jax.ShapeDtypeStruct((chips, 2, rows, width), BF)
    work = sides * 2 * rows * width * 3 * cpad * 4
    return pl.pallas_call(
        lambda *refs: mix_backward_body(cpad, slots, span, edge, *refs),
        grid_spec=pltpu.PrefetchScalarGridSpec(
            num_scalar_prefetch=1,
            grid=(sides,),
            in_specs=[
                main(0),
                main(1),
                pl.BlockSpec((1, edge, cpad), lambda i, r: (side(i, r), 0, 0)),
                pl.BlockSpec((1, 2, rows, width), lambda i, r: (side(i, r), 0, 0, 0)),
                pl.BlockSpec((1, 2 * rows + 2 * edge, 3 * cpad), lambda i, r: (side(i, r), 0, 0)),
                fixed(w_in.shape),
                fixed(taps.shape),
            ],
            out_specs=[
                fixed((width, 3 * chan)),
                pl.BlockSpec((1, 2, rows, width), lambda i, r: (jnp.maximum(i - chips, 0), 0, 0, 0)),
                pl.BlockSpec((1, 2, rows, width), lambda i, r: (jnp.minimum(i, chips - 1), 0, 0, 0)),
                fixed((8, cpad)),
            ],
            scratch_shapes=[pltpu.VMEM((width, 3 * cpad), F32), pltpu.VMEM((2 * rows, 3 * cpad), BF)],
        ),
        out_shape=[
            jax.ShapeDtypeStruct((width, 3 * chan), BF),
            da_shape,
            da_shape,
            jax.ShapeDtypeStruct((8, cpad), F32),
        ],
        compiler_params=pltpu.CompilerParams(vmem_limit_bytes=60 * 2**20),
        cost_estimate=pl.CostEstimate(flops=work, bytes_accessed=40 * 2**20, transcendentals=0),
        name="mix_backward",
    )(nat, do_all, do_all, do_rim, a_all, bcx, w_in, taps)


def attend_body(count, o, w, x, gain, o_cat, h1, a2):
    joined = jnp.concatenate([o[t] for t in range(count)], axis=1)
    o_cat[...] = joined
    total = x[...].astype(F32) + dot(joined, w[...])
    h1[...] = total
    a2[...] = (total * rms_scale(total) * gain[...]).astype(BF)


def attend(o, w_out, x, gain, block):
    count, rows, cpad = o.shape
    width = w_out.shape[1]

    def row(last):
        return pl.BlockSpec((block, last), lambda i: (i, 0))

    def fixed(shape):
        return pl.BlockSpec(shape, lambda i: (0,) * len(shape))

    return pl.pallas_call(
        lambda *refs: attend_body(count, *refs),
        grid=(rows // block,),
        in_specs=[
            pl.BlockSpec((count, block, cpad), lambda i: (0, i, 0)),
            fixed(w_out.shape),
            row(width),
            fixed(gain.shape),
        ],
        out_specs=[row(count * cpad), row(width), row(width)],
        out_shape=[
            jax.ShapeDtypeStruct((rows, count * cpad), BF),
            jax.ShapeDtypeStruct((rows, width), F32),
            jax.ShapeDtypeStruct((rows, width), BF),
        ],
        compiler_params=pltpu.CompilerParams(vmem_limit_bytes=40 * 2**20),
        cost_estimate=pl.CostEstimate(
            flops=2 * rows * width * count * cpad, bytes_accessed=14 * 2**20, transcendentals=0
        ),
        name="attend",
    )(o, w_out, x, gain)


def turn_body(count, terms, *refs):
    da2 = refs[0][0].astype(F32)
    for ref in refs[1:terms]:
        da2 = da2 + ref[0].astype(F32)
    d_out, h1, gain, w, dh1, datt, d_o = refs[terms:]
    values = h1[...]
    grad = d_out[...].astype(F32) + norm_back(da2, values, rms_scale(values), gain[...])
    dh1[...] = grad
    low = grad.astype(BF)
    datt[...] = low
    cpad = w.shape[0] // count
    for t in range(count):
        d_o[t] = dot_nt(low, w[t * cpad : (t + 1) * cpad]).astype(BF)


def turn(terms, d_out, h1, gain, w_out, count, block):
    rows, width = h1.shape
    cpad = w_out.shape[0] // count

    def row(last):
        return pl.BlockSpec((block, last), lambda i: (i, 0))

    def fixed(shape):
        return pl.BlockSpec(shape, lambda i: (0,) * len(shape))

    return pl.pallas_call(
        lambda *refs: turn_body(count, len(terms), *refs),
        grid=(rows // block,),
        in_specs=[pl.BlockSpec((1, block, width), lambda i: (0, i, 0))] * len(terms)
        + [row(width), row(width), fixed(gain.shape), fixed(w_out.shape)],
        out_specs=[row(width), row(width), pl.BlockSpec((count, block, cpad), lambda i: (0, i, 0))],
        out_shape=[
            jax.ShapeDtypeStruct((rows, width), F32),
            jax.ShapeDtypeStruct((rows, width), BF),
            jax.ShapeDtypeStruct((count, rows, cpad), BF),
        ],
        compiler_params=pltpu.CompilerParams(vmem_limit_bytes=40 * 2**20),
        cost_estimate=pl.CostEstimate(
            flops=2 * rows * width * count * cpad, bytes_accessed=20 * 2**20, transcendentals=0
        ),
        name="turn",
    )(*terms, d_out, h1, gain, w_out)


def finish_body(terms, *refs):
    da = refs[0][0].astype(F32)
    for ref in refs[1:terms]:
        da = da + ref[0].astype(F32)
    x, dh1, gain, out = refs[terms:]
    values = x[...].astype(F32)
    out[...] = dh1[...] + norm_back(da, values, rms_scale(values), gain[...])


def finish(terms, x, dh1, gain, block):
    rows, width = dh1.shape
    spec = pl.BlockSpec((block, width), lambda i: (i, 0))
    return pl.pallas_call(
        lambda *refs: finish_body(len(terms), *refs),
        grid=(rows // block,),
        in_specs=[pl.BlockSpec((1, block, width), lambda i: (0, i, 0))] * len(terms)
        + [spec] * 2
        + [pl.BlockSpec(gain.shape, lambda i: (0, 0))],
        out_specs=spec,
        out_shape=jax.ShapeDtypeStruct((rows, width), F32),
        compiler_params=pltpu.CompilerParams(vmem_limit_bytes=60 * 2**20),
        cost_estimate=pl.CostEstimate(flops=rows * width * 8, bytes_accessed=12 * 2**20, transcendentals=0),
        name="finish",
    )(*terms, x, dh1, gain)


def feed_body(hid, hpad, a2, d_out, w_both, w_down, *refs):
    m, d_both, f, da2 = refs[-4:]
    gu = dot(a2[0], w_both[...])
    gate, up = gu[:, :hid], gu[:, hpad : hpad + hid]
    dm = dot_nt(d_out[0], w_down[...])
    sigma = 1.0 / (1.0 + jnp.exp(-gate))
    active = gate * sigma
    inner = (active * up).astype(BF)
    m[0] = inner
    if hpad > hid:
        none = jnp.zeros((gu.shape[0], hpad - hid), BF)
        d_both[0, :, hid:hpad] = none
        d_both[0, :, hpad + hid :] = none
    d_both[0, :, :hid] = (dm * up * (sigma * (1.0 + gate * (1.0 - sigma)))).astype(BF)
    d_both[0, :, hpad : hpad + hid] = (dm * active).astype(BF)
    f[0] = dot(inner, w_down[...]).astype(BF)
    da2[0] = dot_nt(d_both[0], w_both[...]).astype(BF)


def feed(a2_all, d_all, w_both, w_down, first, kept=()):
    blocks, rows, width = a2_all.shape
    half = blocks // 2
    hid, hpad = w_down.shape[0], w_both.shape[1] // 2

    def part(last):
        return pl.BlockSpec((1, rows, last), lambda i: (i + first, 0, 0))

    def fixed(shape):
        return pl.BlockSpec(shape, lambda i: (0,) * len(shape), pipeline_mode=pl.Buffered(1))

    own = pl.BlockSpec((1, rows, width), lambda i: (i, 0, 0))
    return pl.pallas_call(
        lambda *refs: feed_body(hid, hpad, *refs),
        grid=(half,),
        in_specs=[part(width), part(width), fixed(w_both.shape), fixed(w_down.shape)]
        + [pl.BlockSpec(memory_space=pl.ANY)] * len(kept),
        out_specs=[part(hid), part(2 * hpad), own, own],
        out_shape=[
            jax.ShapeDtypeStruct((blocks, rows, hid), BF),
            jax.ShapeDtypeStruct((blocks, rows, 2 * hpad), BF),
            jax.ShapeDtypeStruct((half, rows, width), BF),
            jax.ShapeDtypeStruct((half, rows, width), BF),
        ],
        input_output_aliases={4 + i: i for i in range(len(kept))},
        compiler_params=pltpu.CompilerParams(vmem_limit_bytes=60 * 2**20),
        cost_estimate=pl.CostEstimate(
            flops=half * rows * width * hid * 12, bytes_accessed=40 * 2**20, transcendentals=half * rows * hid
        ),
        name="feed",
    )(a2_all, d_all, w_both, w_down, *kept)


def on_device(
    tokens,
    cotangent,
    lengths,
    in_weight,
    conv_weight,
    out_weight,
    gain_one,
    gain_two,
    gate_weight,
    up_weight,
    down_weight,
):
    nx, nc, nz, ny = (lax.axis_size(name) for name in ("x", "c", "z", "y"))
    sizes = (nx, nc, ny)
    ndp = nx * nc
    slots, span, width = tokens.shape
    conv_weight_early = conv_weight
    rows = slots * span
    own_in = in_weight.shape[0]
    own_hid = down_weight.shape[0]
    chan, hid = nz * own_in, nz * own_hid
    cpad, hpad = up_to(chan + 2, 128), up_to(hid, 128)
    edge = up_to(2 * slots, 16)
    hops = [(dx, dc, dy) for dc in range(nc) for dx in range(nx) for dy in range(ny)]
    sides = ndp
    line = Line(nz)
    row_y = lax.axis_index("y")
    here = [lax.axis_index(name) for name in GROUP]
    place = []
    for i in range(nx):
        for j in range(nc):
            for k in range(ny):
                far = [(to + n - at) % n for to, at, n in zip((i, j, k), here, sizes)]
                place.append((far[1] * nx + far[0]) * ny + far[2])
    place = jnp.stack(place).astype(jnp.int32)
    turn_at = []
    for dx, dc, dy in hops:
        at = [(at + far) % n for at, far, n in zip(here, (dx, dc, dy), sizes)]
        turn_at.append((at[0] * nc + at[1]) * ny + at[2])
    nat = jnp.stack(turn_at).astype(jnp.int32)
    first = (lax.axis_index("z") * ny + row_y) * span
    positions = first + jnp.arange(span, dtype=jnp.int32)
    mask = (positions[None, :] < lengths[:, None]).astype(F32).reshape(rows, 1)
    rim_route = []
    for z in range(nz - 1):
        rim_route += [(z * ny + 1, (z + 1) * ny), ((z + 1) * ny, z * ny + 1)]
    down_route = [(z + 1, z) for z in range(nz - 1)]

    def stack_sides(parts):
        near = stack([parts[h] for h in hops[:sides]], len(hops))
        return stack([parts[h] for h in hops[sides:]], len(hops), sides, near)

    def rim(values, start):
        count, last = values.shape[0], values.shape[-1]
        some = values.reshape(count, slots, span, last)[:, :, start : start + 2].reshape(count, 2 * slots, last)
        return jnp.pad(some, ((0, 0), (0, edge - 2 * slots), (0, 0)))

    x_bf = tokens.reshape(rows, width)
    x = x_bf.astype(F32)
    d_out_bf = (mask * cotangent.reshape(rows, width).astype(F32)).astype(BF)

    hold = lax.optimization_barrier
    plan = shuffle_plan(ndp, nz, ny)

    gains = jnp.stack([gain_one, gain_two], axis=1)
    cut = cut_columns([in_weight], own_in, cpad, plan, gains)
    cut = lax.all_to_all(cut, GROUP, 0, 0, tiled=True).reshape(ndp, ny, own_in, 3 * cpad)
    taps_here = jnp.pad(conv_weight.T, ((0, 0), (0, 128 - conv_weight.shape[0])))
    w_out = line.fetch_all(jnp.concatenate([out_weight, taps_here], axis=1))
    pairs = tokens.reshape(slots, span, width)
    pairs = jnp.where(row_y == 0, pairs[:, :2], pairs[:, -2:]).reshape(2 * slots, width)
    x_rim = lax.ppermute(jnp.pad(pairs, ((0, edge - 2 * slots), (0, 0))), ("z", "y"), rim_route)
    (cut, x_rim), (x_late, gate_late) = after((cut, x_rim), (x_bf, gate_weight))
    x_late = jnp.concatenate([x_late, x_rim], axis=0)

    w_in = lax.all_gather(cut.reshape(ndp, ny * own_in, 3 * cpad), "z", axis=1, tiled=True).reshape(width, 3 * cpad)
    w_out = line.place(w_out, 0).reshape(chan, width + 128)
    taps = w_out[:, width : width + 8].astype(F32).T
    taps = jnp.pad(taps, ((0, 0), (0, cpad - chan)))
    w_out = w_out[:, :width]
    x_all = near_gather(x_late, sizes)
    both = cut_columns([gate_late, up_weight], own_hid, hpad, plan)
    both = lax.all_to_all(both, GROUP, 0, 0, tiled=True).reshape(ndp, ny * own_in, 2 * hpad)
    x_all, both, w_out = hold((x_all, both, w_out))

    w_both = lax.all_gather(both, "z", axis=1, tiled=True).reshape(width, 2 * hpad)
    x_all = far_gather(x_all, sizes)
    gain_a = w_in[:, chan].astype(F32).reshape(1, width)
    gain_b = w_in[:, chan + 1].astype(F32).reshape(1, width)
    x_all, (w_out, d_late) = after(x_all, (w_out, d_out_bf))

    w_out = near_gather(w_out, sizes)
    x_all = stack_sides(x_all)
    d_all = near_gather(d_late, sizes)
    a_all, bcx, o_all = mix_forward(x_all, w_in, gain_a, taps, place, sides, slots, span, edge)
    o_all, w_out = hold((o_all, w_out))
    w_out = diag_gather(w_out, sizes)

    o_own = lax.all_to_all(o_all.reshape(len(hops), rows, cpad), GROUP, 0, 0, tiled=True)
    w_some = cross_gather(w_out, sizes)
    w_out = jnp.zeros((len(hops), cpad, width), BF)
    for i, h in enumerate(hops):
        w_out = lax.dynamic_update_slice(w_out, w_some[h][None], (turn_at[i], 0, 0))
    w_out = w_out.reshape(len(hops) * cpad, width)
    o_own, w_out = hold((o_own, w_out))

    block = rows // 2
    o_cat, h1, a2 = attend(o_own, w_out, x_bf, gain_b, block)
    (_, w_both), down_weight = after((a2, w_both), down_weight)

    w_down = lax.all_gather(down_weight, "z", axis=0, tiled=True)
    a2_all = near_gather(a2, sizes)
    d_all = cross_gather(diag_gather(d_all, sizes), sizes)
    a2_all, d_all = hold((a2_all, d_all))
    d_all = stack([d_all[h] for h in hops])
    a2_all, d_all = hold((diag_gather(a2_all, sizes), d_all))
    a2_all = cross_gather(a2_all, sizes)
    a2_all = stack_sides(a2_all)

    m, d_both, f_far, da_far = feed(a2_all, d_all, w_both, w_down, len(hops) // 2)
    m, d_both, f_near, da_near = feed(a2_all, d_all, w_both, w_down, 0, (m, d_both))
    da2 = GroupSum(da_near, da_far, sizes)
    f = GroupSum(f_near, f_far, sizes)
    d_flat = d_all.reshape(-1, width)
    da2.sum_far()
    da2.total, m = after(da2.total, m)
    da2.send_far()
    down_part = dot_tn(m.reshape(-1, hid), d_flat).astype(BF)
    da2.more, f.cross, down_part = hold((da2.more, f.cross, down_part))

    da2.sum_near()
    da2.total, d_both = after(da2.total, d_both)
    da2.send_near()
    both_part = dot_tn(a2_all.reshape(-1, width), d_both.reshape(-1, 2 * hpad)).astype(BF)
    da2.last, both_part, f.cross = hold((da2.last, both_part, f.cross))
    both_sum = lax.psum_scatter(
        both_part.reshape(ndp, nz * ny * own_in, 2 * hpad), "z", scatter_dimension=1, tiled=True
    )

    f.sum_far()
    da2.last, f.total = hold((da2.last, f.total))
    f.send_far()
    dh1, datt, do_own = turn(da2.terms(), d_out_bf, h1, gain_b, w_out, len(hops), block)
    do_own, datt, f.more = hold((do_own, datt, f.more))

    do_all = lax.all_to_all(do_own, GROUP, 0, 0, tiled=True)
    out_part = dot_tn(o_cat, datt).astype(BF).reshape(len(hops), cpad, width)[:, :chan]
    out_near = jnp.stack([lax.dynamic_index_in_dim(out_part, t, 0, keepdims=False) for t in turn_at[:ndp]], axis=0)
    out_far = jnp.stack([lax.dynamic_index_in_dim(out_part, t, 0, keepdims=False) for t in turn_at[ndp:]], axis=0)
    out = GroupSum(out_near, out_far, sizes)
    f.sum_near()
    do_all, out.cross, f.total = hold((do_all, out.cross, f.total))

    do_rim = lax.ppermute(rim(do_all.reshape(sides, ny, rows, cpad)[:, 0], 0), "z", down_route)
    out.sum_far()
    do_rim, f.total, out.total = hold((do_rim, f.total, out.total))

    f.send_near()
    out.send_far()
    in_part, da_near, da_far, conv_part = mix_backward(
        do_all, do_rim, a_all, bcx, w_in, taps, nat, sides, slots, span, edge, chan
    )
    (in_part, da_near, da_far, conv_part), f.last, out.more = hold(
        ((in_part, da_near, da_far, conv_part), f.last, out.more)
    )

    flat = (ndp, rows, width)
    da = GroupSum(da_near.reshape(flat), da_far.reshape(flat), sizes)
    in_part, both_sum = hold((in_part, both_sum))
    in_sum = lax.psum_scatter(
        in_part.reshape(ndp, nz * ny * own_in, 3 * chan), "z", scatter_dimension=1, tiled=True
    )
    both_sum = lax.all_to_all(both_sum.reshape(ndp * ny, own_in, 2 * hpad), GROUP, 0, 0, tiled=True)
    da.cross = hold(da.cross)

    da.sum_far()
    da.send_far()
    out.sum_near()
    out.send_near()
    da.more = hold(da.more)
    da.sum_near()
    _, in_sum, both_sum, out.last = hold((da.total, in_sum, both_sum, out.last))
    in_sum, down_part = after(in_sum, down_part)
    down_grad = lax.psum_scatter(down_part, "z", scatter_dimension=0, tiled=True)
    da.send_near()
    in_sum = lax.all_to_all(in_sum.reshape(ndp * ny, own_in, 3 * chan), GROUP, 0, 0, tiled=True)
    out_sum = sum(term[0].astype(F32) for term in out.terms()).astype(BF)
    out_grad = line.reduce_direct(out_sum.reshape(nz, own_in, width), 0)
    conv_grad = line.reduce_direct(conv_part[:3, :chan].reshape(3, nz, own_in), 1)
    (gate_grad, up_grad), gain_two_grad = join_columns(
        both_sum, [gate_weight, up_weight], gain_two, own_hid, hpad, plan
    )
    in_sum, da.last, f.last, gate_grad, up_grad = hold((in_sum, da.last, f.last, gate_grad, up_grad))
    total = h1
    for term in f.terms():
        total = total + term[0].astype(F32)
    mixed = (mask * total).astype(BF)

    input_grad = finish(da.terms(), x_bf, dh1, gain_a, block)
    out_grad = sum(term.astype(F32) for term in out_grad)
    conv_grad = sum(conv_grad)
    (in_grad,), gain_one_grad = join_columns(in_sum, [in_weight], gain_one, own_in, chan, plan)
    down_grad = down_grad.astype(F32)
    return (
        mixed.reshape(slots, span, width),
        input_grad.reshape(slots, span, width),
        in_grad,
        conv_grad,
        out_grad,
        gain_one_grad,
        gain_two_grad,
        gate_grad,
        up_grad,
        down_grad,
    )


def solution(mesh):
    dp, seq = mesh.shape["dp"], mesh.shape["seq"]
    fine = Mesh(mesh.devices.reshape(dp // 2, 2, seq // 2, 2), ("x", "c", "z", "y"))
    slot, place = ("x", "c"), ("z", "y")
    every = slot + place
    in_specs = (
        P(slot, place, None),
        P(slot, place, None),
        P(slot),
        P(every, None),
        P(None, every),
        P(every, None),
        P(every),
        P(every),
        P(every, None),
        P(every, None),
        P(every, None),
    )
    out_specs = (
        P(slot, place, None),
        P(slot, place, None),
        P(every, None),
        P(None, every),
        P(every, None),
        P(every),
        P(every),
        P(every, None),
        P(every, None),
        P(every, None),
    )
    return jax.shard_map(
        on_device, mesh=fine, in_specs=in_specs, out_specs=out_specs, check_vma=False
    )
```
